128 devices in a mesh: ex: 16 (over x, y_lo, core), tp: 8 (over y_hi, z).
Axes of the slice: x: 4, y: 4 (y_hi: 2, y_lo: 2; y = y_hi * 2 + y_lo), z: 4, core: 2. Of those that a mesh axis runs over, the one named last changes fastest.
Arguments:
- acts: bfloat16 [12288, 28672], P('ex', 'tp'), may hold values from -20000 to 20000, as said below
- grads: bfloat16 [12288, 8192], P('ex', 'tp'), may hold values from -20000 to 20000, as said below
Outputs:
- kernel: float32 [12288, 3, 768], P(('ex', 'tp'))
The draws below stay inside these ranges and needn't reach their ends.
Inputs may be any that keep to these rules, and one draw needn't show every extreme that they name: `acts`: finite values of order one to some thousands; every row has nonzero entries. `grads`: finite values of order one to some thousands; every row has nonzero entries.
All inputs are finite; a program needn't handle non-finite values.
Results may differ from the reference program's by a relative error of at most 0.00063.
Values may be sent and summed in bfloat16 or wider, within the bound.
A program may use at most 128 MiB of HBM per device.

```python
import jax
import jax.numpy as jnp
from jax import lax

D = 8192
FF = 28672
ROWS = 768
EXAMPLES = 12288
N_EX = 16


factor_count = 2048


def shared_weights(key):
    lead_size = jax.random.uniform(jax.random.fold_in(key, 21), (EXAMPLES, 1), jnp.float32, 0.6, 1.4)
    lead_sign = (2 * jax.random.randint(jax.random.fold_in(key, 22), (EXAMPLES, 1), 0, 2) - 1).astype(jnp.float32)
    spread = jax.random.normal(jax.random.fold_in(key, 23), (EXAMPLES, factor_count), jnp.float32)
    spread = spread * (1.0 / jnp.sqrt(jnp.float32(factor_count)))
    return jnp.concatenate([lead_size * lead_sign, spread], axis=1)


def mixture(key, columns, weights, noise_part, row_top):
    factors = jax.random.normal(jax.random.fold_in(key, 1), (factor_count + 1, columns), jnp.float32)
    structured = jnp.dot(weights, factors, precision=lax.Precision.HIGHEST)
    values = structured + 0.45 * noise_part
    row_scale = jnp.exp(jax.random.uniform(jax.random.fold_in(key, 3), (EXAMPLES, 1), jnp.float32, 0.0, jnp.log(row_top)))
    col_scale = jnp.exp(jax.random.uniform(jax.random.fold_in(key, 4), (1, columns), jnp.float32, 0.0, jnp.log(10.0)))
    trend = jnp.sqrt(1.0 + 2.0 * jnp.arange(columns, dtype=jnp.float32) / columns)
    return (values * row_scale * col_scale * trend[None, :]).astype(jnp.bfloat16)


def draw_acts(key, part):
    weights = shared_weights(key)
    key = jax.random.fold_in(key, 11)
    noise_part = jax.random.normal(jax.random.fold_in(key, 5), (EXAMPLES, FF), jnp.float32)
    return mixture(key, FF, weights, noise_part, 10.0)


def draw_grads(key, part):
    weights = shared_weights(key)
    key = jax.random.fold_in(key, 13)
    noise_part = jax.random.normal(jax.random.fold_in(key, 5), (EXAMPLES, D), jnp.float32)
    return mixture(key, D, weights, noise_part, 10.0)


def setup_inputs(seed: int = 0) -> dict:
    key_list = jax.random.split(jax.random.key(seed), 3)
    acts = draw_acts(jax.random.fold_in(key_list[2], 71), 0)
    grads = draw_grads(jax.random.fold_in(key_list[2], 71), 0)
    return dict(acts=acts, grads=grads)


epsilon = 1e-06

def unit_rows(values):
    wide = values.astype(jnp.float32)
    total = lax.optimization_barrier(jnp.sum(wide * wide, axis=1, keepdims=True))
    return (wide / jnp.sqrt(total + epsilon)).astype(jnp.bfloat16)

def dot_rows(left, right):
    return lax.dot_general(left, right, (((1,), (1,)), ((), ())), preferred_element_type=jnp.float32)

def reference(acts, grads):
    act_unit = unit_rows(acts).reshape(N_EX, ROWS, FF)
    grad_unit = unit_rows(grads).reshape(N_EX, ROWS, D)

    def one_block(block):
        tile_list = []
        for offset in range(3):
            partner = ((block - offset) % N_EX).astype(jnp.int32)
            gram_act = dot_rows(act_unit[block], act_unit[partner])
            gram_grad = dot_rows(grad_unit[block], grad_unit[partner])
            tile_list.append(gram_act * gram_grad)
        return jnp.stack(tile_list, axis=1)
    stacked = lax.map(one_block, jnp.arange(N_EX, dtype=jnp.int32))
    return stacked.reshape(EXAMPLES, 3, ROWS)
```

```python
import functools

import jax
import jax.numpy as jnp
from jax import lax
from jax.experimental import pallas as pl
from jax.experimental.pallas import tpu as pltpu
from jax.sharding import PartitionSpec as P

epsilon = 1e-06
MESH = pl.DeviceIdType.MESH
F32 = jnp.float32
BF16 = jnp.bfloat16

ROWS = 768
SEG = 96
KA, KG = 3584, 1024
HA, HG = KA // 2, KG // 2
NA, NG = 6, 2
CA, CG = ROWS // NA, ROWS // NG
WIDE = ROWS // 2

SCALE, SHIFT = 248.0, 124.0

UNITS = ["dg", "da", "wg", "wa", "c0g", "c1g", "c2g", "c0a", "c1a", "c2a"]
U = {name: i for i, name in enumerate(UNITS)}
SLOT = dict(dg=0, da=1, wg=2, wa=3, c0g=4, c1g=5, c2g=6, c0a=0, c1a=1, c2a=4)


def encode(value):
    power = jnp.exp2(jnp.abs(value) * SCALE - SHIFT)
    return jnp.where(value < 0, -power, power).astype(BF16)


def decode(code):
    wide = code.astype(F32)
    size = jnp.log(jnp.abs(wide)) * (1.4426950408889634 / SCALE) + SHIFT / SCALE
    return jnp.where(wide < 0, -size, size)


def dot_rows(left, right):
    return lax.dot_general(
        left, right, (((1,), (1,)), ((), ())), preferred_element_type=F32
    )


def kernel(
    acts, grads, out, w_a, w_g,
    own_a, own_g, u_a, u_g, tmp, part, z1s, z2s, ys, z1r, z2r, yr, sums, inv,
    own_sem, pair_send_a, pair_send_g, ab_a, ab_g, x_send_a, x_send_g, x_recv_a, x_recv_g,
    c_send_a, c_send_g, c_recv_a, c_recv_g, w_send, w_recv, w_load,
    sum_send, sum_recv, inv_send, inv_recv,
    z1_send, z1_recv, z2_send, z2_recv, y_send, y_recv,
):
    ex, tp = lax.axis_index("ex"), lax.axis_index("tp")
    x, r, c = ex // 4, (ex // 2) % 2, ex % 2
    yh, z = tp // 4, tp % 4
    x_next, x_prev = (x + 1) % 4, (x + 3) % 4
    z_next, z_prev, z_far = (z + 1) % 4, (z + 3) % 4, (z + 2) % 4

    def dev(xx, rr, cc, hh=yh, zz=z):
        return (xx * 4 + rr * 2 + cc, hh * 4 + zz)

    def remote(src, dst, send, recv, device):
        return pltpu.make_async_remote_copy(
            src_ref=src, dst_ref=dst, send_sem=send, recv_sem=recv,
            device_id=device, device_id_type=MESH,
        )

    def arrived(ref, sem):
        pltpu.make_async_copy(ref, ref, sem).wait()

    barrier = pltpu.get_barrier_semaphore()

    def greet(device):
        pl.semaphore_signal(barrier, inc=1, device_id=device, device_id_type=MESH)

    for step in range(1, 8):
        greet((ex, (tp + step) % 8))
    for rr, cc in ((0, 1), (1, 0), (1, 1)):
        greet(dev(x, (r + rr) % 2, (c + cc) % 2))
        greet(dev(x, (r + rr) % 2, (c + cc) % 2, 1 - yh))
    for rr in range(2):
        for cc in range(2):
            greet(dev(x_prev, rr, cc))
    pl.semaphore_wait(barrier, 17)

    pair, mate, ahead = dev(x, 1 - r, c), dev(x, r, 1 - c), dev(x_next, r, c)
    col_a = pl.multiple_of(r * HA, 128), pl.multiple_of((1 - r) * HA, 128)
    col_g = pl.multiple_of(r * HG, 128), pl.multiple_of((1 - r) * HG, 128)
    pltpu.make_async_copy(acts, own_a, own_sem.at[0]).start()
    pltpu.make_async_copy(grads, own_g, own_sem.at[1]).start()

    kinds = {
        0: (grads, u_g, col_g, HG, CG, NG, pair_send_g, ab_g, x_send_g, x_recv_g, c_send_g, c_recv_g),
        1: (acts, u_a, col_a, HA, CA, NA, pair_send_a, ab_a, x_send_a, x_recv_a, c_send_a, c_recv_a),
    }

    def rows_of(kind, k):
        chunk = kinds[kind][4]
        return pl.ds(pl.multiple_of(k * chunk, chunk), chunk)

    def pair_copy(kind, k):
        src, slots, cols, half, _, _, send, recv = kinds[kind][:8]
        rows = rows_of(kind, k)
        return remote(src.at[rows, pl.ds(cols[1], half)], slots.at[r, rows], send.at[k], recv.at[r, k], pair)

    def keep_copy(kind, k):
        src, slots, cols, half, _, _, _, recv = kinds[kind][:8]
        rows = rows_of(kind, k)
        return pltpu.make_async_copy(src.at[rows, pl.ds(cols[0], half)], slots.at[r, rows], recv.at[r, k])

    def x_copy(kind, k, first):
        src, slots, cols, half = kinds[kind][:4]
        send, recv = kinds[kind][8:10]
        rows = rows_of(kind, k)
        source = src.at[rows, pl.ds(cols[0], half)] if first else slots.at[1, rows]
        return remote(source, slots.at[2, rows], send.at[k], recv.at[k], ahead)

    def c_copy(kind, k, which):
        src, slots, cols, half = kinds[kind][:4]
        send, recv = kinds[kind][10:12]
        rows = rows_of(kind, k)
        source = src.at[rows, pl.ds(cols[0], half)] if which == 0 else slots.at[which, rows]
        return remote(source, slots.at[3, rows], send.at[k], recv.at[k], mate)

    def send_first(kind, k):
        pair_copy(kind, k).start()
        keep_copy(kind, k).start()

        @pl.when(r == 1)
        def _():
            x_copy(kind, k, True).start()

            @pl.when(c == 0)
            def _():
                c_copy(kind, k, 0).start()

    for kind in (0, 1):
        @pl.loop(0, kinds[kind][5])
        def _(k):
            send_first(kind, k)

    def w_copies():
        return (
            remote(acts, w_a, w_send.at[0], w_recv.at[0], mate),
            remote(grads, w_g, w_send.at[1], w_recv.at[1], mate),
        )

    @pl.when(c == 0)
    def _():
        for copy in w_copies():
            copy.start()

    def pass_block(kind, k):
        slots, recv = kinds[kind][1], kinds[kind][7]
        rows = rows_of(kind, k)
        arrived(slots.at[1, rows], recv.at[1, k])

        @pl.when(r == 0)
        def _():
            x_copy(kind, k, False).start()

            @pl.when(c == 0)
            def _():
                c_copy(kind, k, 1).start()

        arrived(slots.at[0, rows], recv.at[0, k])

    def pass_far(kind, k):
        slots, recv = kinds[kind][1], kinds[kind][9]
        rows = rows_of(kind, k)
        arrived(slots.at[2, rows], recv.at[k])

        @pl.when(c == 1)
        def _():
            c_copy(kind, k, 2).start()

    def wait_mate(kind, k):
        slots, recv = kinds[kind][1], kinds[kind][11]
        arrived(slots.at[3, rows_of(kind, k)], recv.at[k])

    def put_sums(ref, row, width):
        @pl.loop(0, ROWS // 128)
        def _(i):
            rows = pl.ds(pl.multiple_of(i * 128, 128), 128)
            total = jnp.zeros((128, 128), F32)
            for j in range(width // 128):
                value = ref[rows, 128 * j : 128 * j + 128].astype(F32)
                total += value * value
            sums[tp, row : row + 1, rows] = jnp.sum(total.T, axis=0, keepdims=True)

    sums[tp] = jnp.zeros((8, ROWS), F32)
    arrived(own_g, own_sem.at[1])
    put_sums(own_g, 0, KG)
    arrived(own_a, own_sem.at[0])
    put_sums(own_a, 1, KA)

    def sum_copy(step):
        peer = (tp + step) % 8
        return remote(sums.at[tp], sums.at[tp], sum_send.at[step], sum_recv.at[tp], (ex, peer))

    for step in range(1, 8):
        sum_copy(step).start()
    for step in range(1, 8):
        source = (tp + step) % 8
        arrived(sums.at[source], sum_recv.at[source])
    total = sums[0]
    for i in range(1, 8):
        total += sums[i]
    mine = 2 * r + c
    inv[mine] = 1.0 / jnp.sqrt(total + epsilon)

    def inv_near():
        return [
            remote(inv.at[mine], inv.at[mine], inv_send.at[i], inv_recv.at[mine],
                   dev(x, (r + rr) % 2, (c + cc) % 2))
            for i, (rr, cc) in enumerate(((0, 1), (1, 0), (1, 1)))
        ]
    def inv_far():
        return [
            remote(inv.at[mine], inv.at[4 + c], inv_send.at[3 + 2 * rr + cc], inv_recv.at[4 + c],
                   dev(x_next, rr, cc))
            for rr in range(2) for cc in range(2)
        ]

    near = inv_near()
    for copy in near:
        copy.start()

    @pl.when(r == 1)
    def _():
        for copy in inv_far():
            copy.start()

    pass_block(0, 0)

    def scale_rows(src, dst, block, row, start, count, width):
        @pl.loop(0, count // 128)
        def _(i):
            rows = pl.ds(pl.multiple_of(i * 128, 128), 128)
            lanes = pl.ds(pl.multiple_of(start + i * 128, 128), 128)
            col = jnp.broadcast_to(inv[block, row : row + 1, lanes], (128, 128)).T
            for j in range(width // 128):
                cols = slice(128 * j, 128 * j + 128)
                dst[rows, cols] = (src[rows, cols].astype(F32) * col).astype(BF16)

    def put_cols(unit, left, right, n):
        for m in range(2):
            block = dot_rows(left[WIDE * m : WIDE * m + WIDE, :], right[...])
            part[SLOT[unit], 4 * m : 4 * m + 4, :, pl.ds(pl.multiple_of(n * 256, 256), 256)] = (
                block.reshape(4, SEG, 256)
            )

    def put_rows(unit, left, right, m):
        for n in range(3):
            block = dot_rows(left[...], right[256 * n : 256 * n + 256, :])
            part[SLOT[unit], pl.ds(4 * m, 4), :, 256 * n : 256 * n + 256] = block.reshape(4, SEG, 256)

    def z1_copies(unit):
        u, s = U[unit], SLOT[unit]
        return (
            remote(z1s.at[s, 0], z1r.at[u, 0], z1_send.at[u, 0], z1_recv.at[u, 0], (ex, yh * 4 + z_next)),
            remote(z1s.at[s, 1], z1r.at[u, 1], z1_send.at[u, 1], z1_recv.at[u, 1], (ex, yh * 4 + z_prev)),
        )

    def z2_copies(unit):
        u, s = U[unit], SLOT[unit]
        return (
            remote(z2s.at[s, 0], z2r.at[u, 0], z2_send.at[u, 0], z2_recv.at[u, 0], (ex, yh * 4 + z_next)),
            remote(z2s.at[s, 1], z2r.at[u, 1], z2_send.at[u, 1], z2_recv.at[u, 1], (ex, yh * 4 + z_prev)),
        )

    def blocks(body):
        @pl.loop(0, 6)
        def _(i):
            body(i // 3, pl.ds(pl.multiple_of((i % 3) * 32, 32), 32))

    def z1(unit):
        s = SLOT[unit]

        def body(h, rows):
            z1s[s, 0, h, rows] = encode(part[s, h * 4 + z_far, rows, :WIDE])
            z1s[s, 1, h, rows] = encode(part[s, h * 4 + z_far, rows, WIDE:])

        blocks(body)
        for copy in z1_copies(unit):
            copy.start()

    def z2(unit):
        u, s = U[unit], SLOT[unit]
        for i in range(2):
            arrived(z1r.at[u, i], z1_recv.at[u, i])

        def body(h, rows):
            z2s[s, 0, h, rows, :WIDE] = encode(part[s, h * 4 + z_next, rows, :WIDE] + decode(z1r[u, 0, h, rows]))
            z2s[s, 0, h, rows, WIDE:] = encode(part[s, h * 4 + z_next, rows, WIDE:])
            z2s[s, 1, h, rows, :WIDE] = encode(part[s, h * 4 + z_prev, rows, :WIDE])
            z2s[s, 1, h, rows, WIDE:] = encode(part[s, h * 4 + z_prev, rows, WIDE:] + decode(z1r[u, 1, h, rows]))

        blocks(body)
        for copy in z2_copies(unit):
            copy.start()

    def target(unit):
        if unit[0] == "d":
            return r, c, 8 + yh, yh == yh
        if unit[0] == "w":
            return r, c, 4 + yh, yh == yh
        source = r * 2 + yh
        if unit[:2] == "c0":
            return 0, c, source, r == 0
        if unit[:2] == "c1":
            return 1, c, source, r == 1
        return c, 0, 4 + source, jnp.logical_and(r == 0, c == 0)

    def y_copy(unit, h):
        u, s, kind = U[unit], SLOT[unit], int(unit[-1] == "a")
        rr, cc, slot, _ = target(unit)
        return remote(ys.at[s, h], yr.at[kind, slot], y_send.at[u, h], y_recv.at[kind, slot], dev(x, rr, cc, h))

    def here(unit, h):
        return jnp.logical_and(target(unit)[3], yh == h)

    def z3(unit):
        u, s, kind = U[unit], SLOT[unit], int(unit[-1] == "a")
        for i in range(2):
            arrived(z2r.at[u, i], z2_recv.at[u, i])

        slot = target(unit)[2]

        def body(h, rows):
            total = part[s, h * 4 + z, rows, :] + decode(z2r[u, 0, h, rows]) + decode(z2r[u, 1, h, rows])
            code = encode(total)
            stays = here(unit, h)

            @pl.when(stays)
            def _():
                yr[kind, slot, rows] = code

            @pl.when(jnp.logical_not(stays))
            def _():
                ys[s, h, rows] = code

        blocks(body)
        for h in range(2):
            @pl.when(jnp.logical_not(here(unit, h)))
            def _():
                y_copy(unit, h).start()

    def sent(unit):
        for copy in z1_copies(unit) + z2_copies(unit):
            copy.wait_send()
        for h in range(2):
            @pl.when(jnp.logical_not(here(unit, h)))
            def _():
                y_copy(unit, h).wait_send()

    for i in range(3):
        rr, cc = ((0, 1), (1, 0), (1, 1))[i]
        block = 2 * ((r + rr) % 2) + (c + cc) % 2
        arrived(inv.at[block], inv_recv.at[block])
    for block in (4, 5):
        arrived(inv.at[block], inv_recv.at[block])

    scale_rows(own_g, own_g, mine, 0, 0, ROWS, KG)
    scale_rows(own_a, own_a, mine, 1, 0, ROWS, KA)

    @pl.loop(0, 3)
    def _(n):
        rows = pl.ds(pl.multiple_of(n * 256, 256), 256)
        put_cols("dg", own_g, own_g.at[rows], n)
        put_cols("da", own_a, own_a.at[rows], n)

    z1("dg")
    z1("da")
    pass_block(0, 1)

    @pl.when(c == 1)
    def _():
        arrived(w_a, w_recv.at[0])
        arrived(w_g, w_recv.at[1])

        @pl.loop(0, 3)
        def _(n):
            rows = pl.ds(pl.multiple_of(n * 256, 256), 256)
            wide, narrow = tmp.at[pl.ds(0, 256)], tmp.at[pl.ds(0, 256), pl.ds(0, KG)]
            load = pltpu.make_async_copy(w_g.at[rows], narrow, w_load)
            load.start()
            load.wait()
            scale_rows(narrow, narrow, 2 * r, 0, n * 256, 256, KG)
            put_cols("wg", own_g, narrow, n)
            load = pltpu.make_async_copy(w_a.at[rows], wide, w_load)
            load.start()
            load.wait()
            scale_rows(wide, wide, 2 * r, 1, n * 256, 256, KA)
            put_cols("wa", own_a, wide, n)

        z1("wg")
        z1("wa")

    spans = {0: (u_g, HG, "g"), 1: (u_a, HA, "a")}
    inv_of = {1: 2 + c, 2: 4 + c, 3: 5 - 3 * c}

    def cols_tile(unit, kind, slot):
        slots, half, _ = spans[kind]

        @pl.loop(0, 3)
        def _(n):
            rows = pl.ds(pl.multiple_of(n * 256, 256), 256)
            right = tmp.at[pl.ds(0, 256), pl.ds(0, half)]
            scale_rows(slots.at[slot, rows], right, inv_of[slot], kind, n * 256, 256, half)
            put_cols(unit, slots.at[0], right, n)

    def rows_tile(unit, kind, slot):
        slots, half, _ = spans[kind]

        @pl.loop(0, 2)
        def _(m):
            rows = pl.ds(pl.multiple_of(m * WIDE, WIDE), WIDE)
            left = tmp.at[pl.ds(0, WIDE), pl.ds(0, half)]
            scale_rows(slots.at[slot, rows], left, inv_of[slot], kind, m * WIDE, WIDE, half)
            put_rows(unit, left, slots.at[0], m)

    def scale_a(kind, k):
        slots, half, _ = spans[kind]
        rows, count = rows_of(kind, k), kinds[kind][4]
        block = slots.at[0, rows]
        scale_rows(block, block, c, kind, k * count, count, half)

    def mate_tile(unit, kind):
        @pl.when(c == 0)
        def _():
            cols_tile(unit, kind, 3)

        @pl.when(c == 1)
        def _():
            rows_tile(unit, kind, 3)

    def step(k):
        pass_block(1, k)
        scale_a(1, k)
        if k:
            pass_far(1, k - 1)

    pass_far(0, 0)
    step(0)
    z2("dg")
    z2("da")
    scale_a(0, 0)
    scale_a(0, 1)
    rows_tile("c1g", 0, 1)
    z1("c1g")
    pass_far(0, 1)
    cols_tile("c0g", 0, 2)
    z1("c0g")
    step(1)
    for k in range(NG):
        wait_mate(0, k)
    mate_tile("c2g", 0)
    z1("c2g")
    z3("dg")
    z3("da")
    step(2)

    @pl.when(c == 1)
    def _():
        z2("wg")
        z2("wa")

    z2("c1g")
    z2("c0g")
    z2("c2g")
    step(3)

    @pl.when(c == 1)
    def _():
        z3("wg")
        z3("wa")

    z3("c1g")
    z3("c0g")
    step(4)
    z3("c2g")
    sent("dg")
    sent("da")
    sent("c0g")
    step(5)
    rows_tile("c1a", 1, 1)
    z1("c1a")
    pass_far(1, 5)
    cols_tile("c0a", 1, 2)
    z1("c0a")
    z2("c1a")
    for k in range(NA):
        wait_mate(1, k)
    mate_tile("c2a", 1)
    z1("c2a")
    z2("c0a")
    z3("c1a")
    z2("c2a")
    z3("c0a")
    z3("c2a")

    def collect(kind, slot, stored):
        @pl.when(jnp.logical_not(stored))
        def _():
            arrived(yr.at[kind, slot], y_recv.at[kind, slot])

    for kind in range(2):
        for slot in range(4):
            collect(kind, slot, slot == 2 * r + yh)
        for h in range(2):
            collect(kind, 8 + h, h == yh)
            collect(kind, 4 + h, jnp.logical_and(h == yh, 2 * r + c != 2))
            collect(kind, 6 + h, c == 1)

    def product(index, slots):
        @pl.loop(0, 3)
        def _(i):
            rows = pl.ds(pl.multiple_of(i * 32, 32), 32)
            grams = []
            for kind in range(2):
                gram = decode(yr[kind, slots[0], rows])
                for slot in slots[1:]:
                    gram += decode(yr[kind, slot, rows])
                grams.append(gram)
            out[index, rows] = grams[0] * grams[1]

    product(0, (8, 9))
    product(2, (0, 1, 2, 3))

    @pl.when(c == 0)
    def _():
        product(1, (4, 5, 6, 7))

    @pl.when(c == 1)
    def _():
        product(1, (4, 5))

    for kind in (0, 1):
        @pl.loop(0, kinds[kind][5])
        def _(k):
            pair_copy(kind, k).wait_send()
            x_copy(kind, k, False).wait_send()
            c_copy(kind, k, 1).wait_send()

    @pl.when(c == 0)
    def _():
        for copy in w_copies():
            copy.wait_send()

    for step_ in range(1, 8):
        sum_copy(step_).wait_send()
    for copy in near:
        copy.wait_send()

    @pl.when(r == 1)
    def _():
        for copy in inv_far():
            copy.wait_send()

    @pl.when(c == 1)
    def _():
        sent("wg")
        sent("wa")

    for unit in ("c1g", "c2g", "c0a", "c1a", "c2a"):
        sent(unit)


def on_device(acts, grads):
    dma = pltpu.SemaphoreType.DMA
    n = len(UNITS)
    slots = 7
    any_space = pl.BlockSpec(memory_space=pl.ANY)
    result = pl.pallas_call(
        kernel,
        out_shape=(
            jax.ShapeDtypeStruct((3, SEG, ROWS), F32),
            jax.ShapeDtypeStruct((ROWS, KA), BF16),
            jax.ShapeDtypeStruct((ROWS, KG), BF16),
        ),
        in_specs=[any_space, any_space],
        out_specs=(pl.BlockSpec(memory_space=pltpu.VMEM), any_space, any_space),
        scratch_shapes=[
            pltpu.VMEM((ROWS, KA), BF16),
            pltpu.VMEM((ROWS, KG), BF16),
            pltpu.VMEM((4, ROWS, HA), BF16),
            pltpu.VMEM((4, ROWS, HG), BF16),
            pltpu.VMEM((WIDE, KA), BF16),
            pltpu.VMEM((slots, 8, SEG, ROWS), F32),
            pltpu.VMEM((slots, 2, 2, SEG, WIDE), BF16),
            pltpu.VMEM((slots, 2, 2, SEG, ROWS), BF16),
            pltpu.VMEM((slots, 2, SEG, ROWS), BF16),
            pltpu.VMEM((n, 2, 2, SEG, WIDE), BF16),
            pltpu.VMEM((n, 2, 2, SEG, ROWS), BF16),
            pltpu.VMEM((2, 10, SEG, ROWS), BF16),
            pltpu.VMEM((8, 8, ROWS), F32),
            pltpu.VMEM((6, 8, ROWS), F32),
            dma((2,)), dma((NA,)), dma((NG,)), dma((2, NA)), dma((2, NG)),
            dma((NA,)), dma((NG,)), dma((NA,)), dma((NG,)),
            dma((NA,)), dma((NG,)), dma((NA,)), dma((NG,)),
            dma((2,)), dma((2,)), dma,
            dma((8,)), dma((8,)), dma((7,)), dma((6,)),
            dma((n, 2)), dma((n, 2)), dma((n, 2)), dma((n, 2)), dma((n, 2)), dma((2, 10)),
        ],
        compiler_params=pltpu.CompilerParams(
            collective_id=0, has_side_effects=True, vmem_limit_bytes=64 * 1024 * 1024 - 65536
        ),
        cost_estimate=pl.CostEstimate(
            flops=2 * 3 * ROWS * ROWS * (KA + KG), bytes_accessed=4 * ROWS * (KA + KG), transcendentals=0
        ),
    )(acts, grads)
    return jnp.transpose(result[0], (1, 0, 2))


def solution(mesh):
    placed = (P("ex", "tp"), P("ex", "tp"))
    return jax.shard_map(
        on_device,
        mesh=mesh,
        in_specs=placed,
        out_specs=P(("ex", "tp"), None, None),
        check_vma=False,
    )
```

```python
import functools

import jax
import jax.numpy as jnp
from jax import lax
from jax.experimental import pallas as pl
from jax.experimental.pallas import tpu as pltpu
from jax.sharding import PartitionSpec as P

epsilon = 1e-06
MESH = pl.DeviceIdType.MESH
F32 = jnp.float32
BF16 = jnp.bfloat16

ROWS = 768
SEG = 96
KA, KG = 3584, 1024
HA, HG = KA // 2, KG // 2
NA, NG = 12, 4
WINDOW = 3
LAG = 3
CA, CG = ROWS // NA, ROWS // NG
WIDE = ROWS // 2

SCALE, SHIFT = 248.0, 124.0

UNITS = ["dg", "da", "wg", "wa", "c0g", "c1g", "c2g", "c0a", "c1a", "c2a"]
U = {name: i for i, name in enumerate(UNITS)}
SLOT = dict(dg=0, da=1, wg=2, wa=3, c0g=4, c1g=5, c2g=6, c0a=4, c1a=1, c2a=0)


def encode(value):
    power = jnp.exp2(jnp.abs(value) * SCALE - SHIFT)
    return jnp.where(value < 0, -power, power).astype(BF16)


def decode(code):
    wide = code.astype(F32)
    size = jnp.log(jnp.abs(wide)) * (1.4426950408889634 / SCALE) + SHIFT / SCALE
    return jnp.where(wide < 0, -size, size)


def dot_rows(left, right):
    return lax.dot_general(
        left, right, (((1,), (1,)), ((), ())), preferred_element_type=F32
    )


def kernel(
    acts, grads, out, w_a, w_g,
    own_a, own_g, u_a, u_g, tmp, part, z1s, z2s, ys, z1r, z2r, yr, sums, inv,
    own_sem, keep_sem, pair_send_a, pair_send_g, ab_a, ab_g, x_send_a, x_send_g, x_recv_a, x_recv_g,
    c_send_a, c_send_g, c_recv_a, c_recv_g, w_send, w_recv, w_load,
    sum_send, sum_recv, inv_send, inv_recv,
    z1_send, z1_recv, z2_send, z2_recv, y_send, y_recv,
):
    ex, tp = lax.axis_index("ex"), lax.axis_index("tp")
    x, r, c = ex // 4, (ex // 2) % 2, ex % 2
    yh, z = tp // 4, tp % 4
    x_next, x_prev = (x + 1) % 4, (x + 3) % 4
    z_next, z_prev, z_far = (z + 1) % 4, (z + 3) % 4, (z + 2) % 4

    def dev(xx, rr, cc, hh=yh, zz=z):
        return (xx * 4 + rr * 2 + cc, hh * 4 + zz)

    def remote(src, dst, send, recv, device):
        return pltpu.make_async_remote_copy(
            src_ref=src, dst_ref=dst, send_sem=send, recv_sem=recv,
            device_id=device, device_id_type=MESH,
        )

    def arrived(ref, sem):
        pltpu.make_async_copy(ref, ref, sem).wait()

    barrier = pltpu.get_barrier_semaphore()

    def greet(device):
        pl.semaphore_signal(barrier, inc=1, device_id=device, device_id_type=MESH)

    for step in range(1, 8):
        greet((ex, (tp + step) % 8))
    for rr, cc in ((0, 1), (1, 0), (1, 1)):
        greet(dev(x, (r + rr) % 2, (c + cc) % 2))
        greet(dev(x, (r + rr) % 2, (c + cc) % 2, 1 - yh))
    for rr in range(2):
        for cc in range(2):
            greet(dev(x_prev, rr, cc))
    pl.semaphore_wait(barrier, 17)

    pair, mate, ahead = dev(x, 1 - r, c), dev(x, r, 1 - c), dev(x_next, r, c)
    col_a = pl.multiple_of(r * HA, 128), pl.multiple_of((1 - r) * HA, 128)
    col_g = pl.multiple_of(r * HG, 128), pl.multiple_of((1 - r) * HG, 128)
    pltpu.make_async_copy(acts, own_a, own_sem.at[0]).start()
    pltpu.make_async_copy(grads, own_g, own_sem.at[1]).start()

    kinds = {
        0: (grads, u_g, col_g, HG, CG, NG, pair_send_g, ab_g, x_send_g, x_recv_g, c_send_g, c_recv_g),
        1: (acts, u_a, col_a, HA, CA, NA, pair_send_a, ab_a, x_send_a, x_recv_a, c_send_a, c_recv_a),
    }
    order = [(0, k) for k in range(NG)] + [(1, k) for k in range(NA)]

    def rows_of(kind, k):
        chunk = kinds[kind][4]
        return pl.ds(k * chunk if isinstance(k, int) else pl.multiple_of(k * chunk, chunk), chunk)

    def pair_copy(kind, k):
        src, slots, cols, half, _, _, send, recv = kinds[kind][:8]
        rows = rows_of(kind, k)
        return remote(src.at[rows, pl.ds(cols[1], half)], slots.at[r, rows], send.at[k], recv.at[k], pair)

    def keep_copy(kind):
        src, slots, cols, half = kinds[kind][:4]
        return pltpu.make_async_copy(src.at[:, pl.ds(cols[0], half)], slots.at[r], keep_sem.at[kind])

    def x_copy(kind, k, first):
        src, slots, cols, half = kinds[kind][:4]
        send, recv = kinds[kind][8:10]
        rows = rows_of(kind, k)
        source = src.at[rows, pl.ds(cols[0], half)] if first else slots.at[1, rows]
        return remote(source, slots.at[2, rows], send.at[k], recv.at[k], ahead)

    def c_copy(kind, k, which):
        src, slots, cols, half = kinds[kind][:4]
        send, recv = kinds[kind][10:12]
        rows = rows_of(kind, k)
        source = src.at[rows, pl.ds(cols[0], half)] if which == 0 else slots.at[which, rows]
        return remote(source, slots.at[3, rows], send.at[k], recv.at[k], mate)

    def launch(q):
        kind, k = order[q]
        pair_copy(kind, k).start()

        @pl.when(r == 1)
        def _():
            x_copy(kind, k, True).start()

    for q in range(WINDOW):
        launch(q)
    for kind in (0, 1):
        keep_copy(kind).start()

        @pl.when(jnp.logical_and(r == 1, c == 0))
        def _():
            @pl.loop(0, kinds[kind][5])
            def _(k):
                c_copy(kind, k, 0).start()

    def w_copies():
        return (
            remote(acts, w_a, w_send.at[0], w_recv.at[0], mate),
            remote(grads, w_g, w_send.at[1], w_recv.at[1], mate),
        )

    @pl.when(c == 0)
    def _():
        for copy in w_copies():
            copy.start()

    def serve(q):
        kind, k = order[q]
        slots, recv = kinds[kind][1], kinds[kind][7]
        rows = rows_of(kind, k)
        pair_copy(kind, k).wait_send()
        if q + WINDOW < len(order):
            launch(q + WINDOW)
        arrived(slots.at[1 - r, rows], recv.at[k])

        @pl.when(r == 0)
        def _():
            x_copy(kind, k, False).start()

            @pl.when(c == 0)
            def _():
                c_copy(kind, k, 1).start()

        if q >= LAG:
            pass_far(q - LAG)

    def pass_far(q):
        kind, k = order[q]
        slots, recv = kinds[kind][1], kinds[kind][9]
        rows = rows_of(kind, k)
        arrived(slots.at[2, rows], recv.at[k])

        @pl.when(c == 1)
        def _():
            c_copy(kind, k, 2).start()

    def wait_mate(kind, first, last):
        slots, recv = kinds[kind][1], kinds[kind][11]
        for k in range(first, last):
            arrived(slots.at[3, rows_of(kind, k)], recv.at[k])

    def put_sums(ref, row, width):
        @pl.loop(0, ROWS // 128)
        def _(i):
            rows = pl.ds(pl.multiple_of(i * 128, 128), 128)
            total = jnp.zeros((128, 128), F32)
            for j in range(width // 128):
                value = ref[rows, 128 * j : 128 * j + 128].astype(F32)
                total += value * value
            sums[tp, row : row + 1, rows] = jnp.sum(total.T, axis=0, keepdims=True)

    sums[tp] = jnp.zeros((8, ROWS), F32)
    arrived(own_g, own_sem.at[1])
    put_sums(own_g, 0, KG)
    arrived(own_a, own_sem.at[0])
    put_sums(own_a, 1, KA)

    def sum_copy(step):
        peer = (tp + step) % 8
        return remote(sums.at[tp], sums.at[tp], sum_send.at[step], sum_recv.at[tp], (ex, peer))

    for step in range(1, 8):
        sum_copy(step).start()
    serve(0)
    for step in range(1, 8):
        source = (tp + step) % 8
        arrived(sums.at[source], sum_recv.at[source])
    total = sums[0]
    for i in range(1, 8):
        total += sums[i]
    mine = 2 * r + c
    inv[mine] = 1.0 / jnp.sqrt(total + epsilon)

    def inv_near():
        return [
            remote(inv.at[mine], inv.at[mine], inv_send.at[i], inv_recv.at[mine],
                   dev(x, (r + rr) % 2, (c + cc) % 2))
            for i, (rr, cc) in enumerate(((0, 1), (1, 0), (1, 1)))
        ]
    def inv_far():
        return [
            remote(inv.at[mine], inv.at[4 + c], inv_send.at[3 + 2 * rr + cc], inv_recv.at[4 + c],
                   dev(x_next, rr, cc))
            for rr in range(2) for cc in range(2)
        ]

    near = inv_near()
    for copy in near:
        copy.start()

    @pl.when(r == 1)
    def _():
        for copy in inv_far():
            copy.start()

    serve(1)

    def scale_rows(src, dst, block, row, start, count, width):
        @pl.loop(0, count // 128)
        def _(i):
            rows = pl.ds(pl.multiple_of(i * 128, 128), 128)
            lanes = pl.ds(pl.multiple_of(start + i * 128, 128), 128)
            col = jnp.broadcast_to(inv[block, row : row + 1, lanes], (128, 128)).T
            for j in range(width // 128):
                cols = slice(128 * j, 128 * j + 128)
                dst[rows, cols] = (src[rows, cols].astype(F32) * col).astype(BF16)

    def put_cols(unit, left, right, n):
        for m in range(2):
            block = dot_rows(left[WIDE * m : WIDE * m + WIDE, :], right[...])
            part[SLOT[unit], 4 * m : 4 * m + 4, :, pl.ds(pl.multiple_of(n * 256, 256), 256)] = (
                block.reshape(4, SEG, 256)
            )

    def by_rows(unit):
        if unit[:2] == "c0":
            return 0
        if unit[:2] == "c1":
            return 1 - r
        if unit[:2] == "c2":
            return c * (1 - r)
        return 1

    def quarter(unit, i, d):
        flag = by_rows(unit)
        h = flag * i + (1 - flag) * d
        n = flag * d + (1 - flag) * i
        return h, pl.ds(pl.multiple_of(n * WIDE, WIDE), WIDE), n

    z_peers = (ex, yh * 4 + z_next), (ex, yh * 4 + z_prev)

    def z1_copies(unit, i):
        u, s = U[unit], SLOT[unit]
        return [
            remote(z1s.at[s, i, d], z1r.at[u, i, d], z1_send.at[u, i, d], z1_recv.at[u, i, d], z_peers[d])
            for d in range(2)
        ]

    def z2_copies(unit, i):
        u, s = U[unit], SLOT[unit]
        return [
            remote(z2s.at[s, i, d], z2r.at[u, i, d], z2_send.at[u, i, d], z2_recv.at[u, i, d], z_peers[d])
            for d in range(2)
        ]

    def blocks(body):
        @pl.loop(0, 3)
        def _(k):
            body(pl.ds(pl.multiple_of(k * 32, 32), 32))

    def z1(unit, i):
        s = SLOT[unit]

        def body(rows):
            for d in range(2):
                h, cols, _ = quarter(unit, i, d)
                z1s[s, i, d, rows] = encode(part[s, h * 4 + z_far, rows, cols])

        blocks(body)
        for copy in z1_copies(unit, i):
            copy.start()

    def z2(unit, i):
        u, s = U[unit], SLOT[unit]
        for d in range(2):
            arrived(z1r.at[u, i, d], z1_recv.at[u, i, d])

        def body(rows):
            for d in range(2):
                h, cols, _ = quarter(unit, i, d)
                for way, to in ((0, z_next), (1, z_prev)):
                    value = part[s, h * 4 + to, rows, cols]
                    if way == d:
                        value += decode(z1r[u, i, d, rows])
                    z2s[s, i, way, d, rows] = encode(value)

        blocks(body)
        for copy in z2_copies(unit, i):
            copy.start()

    def target(unit):
        if unit[0] == "d":
            return r, c, 8 + yh, yh == yh
        if unit[0] == "w":
            return r, c, 4 + yh, yh == yh
        source = r * 2 + yh
        if unit[:2] == "c0":
            return 0, c, source, r == 0
        if unit[:2] == "c1":
            return 1, c, source, r == 1
        return c, 0, 4 + source, jnp.logical_and(r == 0, c == 0)

    def here(unit, h):
        return jnp.logical_and(target(unit)[3], yh == h)

    def y_copy(unit, i, d):
        u, s, kind = U[unit], SLOT[unit], int(unit[-1] == "a")
        rr, cc, slot, _ = target(unit)
        h, cols, n = quarter(unit, i, d)
        return remote(
            ys.at[s, i, d], yr.at[kind, slot, n], y_send.at[u, i, d], y_recv.at[kind, slot, n],
            dev(x, rr, cc, h),
        )

    def z3(unit, i):
        u, s, kind = U[unit], SLOT[unit], int(unit[-1] == "a")
        for d in range(2):
            arrived(z2r.at[u, i, d], z2_recv.at[u, i, d])
        slot = target(unit)[2]

        def body(rows):
            for d in range(2):
                h, cols, n = quarter(unit, i, d)
                total = part[s, h * 4 + z, rows, cols]
                total += decode(z2r[u, i, 0, d, rows]) + decode(z2r[u, i, 1, d, rows])
                code = encode(total)
                stays = here(unit, h)

                @pl.when(stays)
                def _():
                    yr[kind, slot, n, rows] = code

                @pl.when(jnp.logical_not(stays))
                def _():
                    ys[s, i, d, rows] = code

        blocks(body)
        for d in range(2):
            @pl.when(jnp.logical_not(here(unit, quarter(unit, i, d)[0])))
            def _():
                y_copy(unit, i, d).start()

    def sent(unit):
        for i in range(2):
            for copy in z1_copies(unit, i) + z2_copies(unit, i):
                copy.wait_send()
            for d in range(2):
                @pl.when(jnp.logical_not(here(unit, quarter(unit, i, d)[0])))
                def _():
                    y_copy(unit, i, d).wait_send()

    def both(step, *units):
        for unit in units:
            for i in range(2):
                step(unit, i)

    def on_core(core, step, *units):
        @pl.when(c == core)
        def _():
            both(step, *units)

    for i in range(3):
        rr, cc = ((0, 1), (1, 0), (1, 1))[i]
        block = 2 * ((r + rr) % 2) + (c + cc) % 2
        arrived(inv.at[block], inv_recv.at[block])
    for block in (4, 5):
        arrived(inv.at[block], inv_recv.at[block])

    serve(2)
    scale_rows(own_g, own_g, mine, 0, 0, ROWS, KG)
    scale_rows(own_a, own_a, mine, 1, 0, ROWS, KA)
    serve(3)

    @pl.loop(0, 3)
    def _(n):
        rows = pl.ds(pl.multiple_of(n * 256, 256), 256)
        put_cols("dg", own_g, own_g.at[rows], n)
        put_cols("da", own_a, own_a.at[rows], n)

    both(z1, "dg", "da")
    serve(4)
    for kind in (0, 1):
        arrived(kinds[kind][1].at[r], keep_sem.at[kind])

    spans = {0: (u_g, HG), 1: (u_a, HA)}
    inv_of = {1: 2 + c, 2: 4 + c, 3: 5 - 3 * c}

    def half_rows(i):
        return pl.ds(i * WIDE if isinstance(i, int) else pl.multiple_of(i * WIDE, WIDE), WIDE)

    def tile(unit, i, slot, a_left):
        kind = int(unit[-1] == "a")
        slots, half = spans[kind]
        scaled = tmp.at[pl.ds(0, WIDE), pl.ds(0, half)]

        @pl.loop(0, 2)
        def _(j):
            h, cols, n = quarter(unit, i, j)
            side = n if a_left else h
            stale = j == 0 if a_left else jnp.logical_or(j == 0, by_rows(unit) == 0)

            @pl.when(stale)
            def _():
                scale_rows(slots.at[slot, half_rows(side)], scaled, inv_of[slot], kind, side * WIDE, WIDE, half)

            fixed = slots[0, half_rows(h if a_left else n), :]
            other = scaled[...]
            block = dot_rows(fixed, other) if a_left else dot_rows(other, fixed)
            part[SLOT[unit], pl.ds(4 * h, 4), :, cols] = block.reshape(4, SEG, WIDE)

    def scale_a(kind, i):
        slots, half = spans[kind]
        block = slots.at[0, half_rows(i)]
        scale_rows(block, block, c, kind, i * WIDE, WIDE, half)

    def tile_b(unit, i):
        tile(unit, i, 1, False)
        z1(unit, i)

    def tile_p(unit, i):
        tile(unit, i, 2, True)
        z1(unit, i)

    def tile_x(unit, i, core):
        tile(unit, i, 3, core == 0)
        z1(unit, i)

    scale_a(0, 0)
    scale_a(0, 1)
    both(tile_b, "c1g")
    serve(5)

    @pl.when(c == 1)
    def _():
        arrived(w_a, w_recv.at[0])
        arrived(w_g, w_recv.at[1])

        @pl.loop(0, 3)
        def _(n):
            rows = pl.ds(pl.multiple_of(n * 256, 256), 256)
            wide, narrow = tmp.at[pl.ds(0, 256)], tmp.at[pl.ds(0, 256), pl.ds(0, KG)]
            load = pltpu.make_async_copy(w_g.at[rows], narrow, w_load)
            load.start()
            load.wait()
            scale_rows(narrow, narrow, 2 * r, 0, n * 256, 256, KG)
            put_cols("wg", own_g, narrow, n)
            load = pltpu.make_async_copy(w_a.at[rows], wide, w_load)
            load.start()
            load.wait()
            scale_rows(wide, wide, 2 * r, 1, n * 256, 256, KA)
            put_cols("wa", own_a, wide, n)

        both(z1, "wg", "wa")

    serve(6)
    both(z2, "dg", "da")
    serve(7)
    both(tile_p, "c0g")
    wait_mate(0, 0, NG)
    for core in range(2):
        @pl.when(c == core)
        def _():
            for i in range(2):
                tile_x("c2g", i, core)

    both(z3, "dg", "da")
    serve(8)
    on_core(1, z2, "wg", "wa")
    both(z2, "c1g")
    sent("dg")
    sent("da")
    serve(9)

    scale_a(1, 0)

    @pl.when(r == 0)
    def _():
        scale_a(1, 1)

    tile_b("c1a", 0)
    both(z2, "c0g", "c2g")
    serve(10)
    on_core(1, z3, "wg", "wa")
    both(z3, "c1g", "c0g")
    serve(11)

    @pl.when(c == 1)
    def _():
        wait_mate(1, 0, NA // 2)

        @pl.when(r == 1)
        def _():
            wait_mate(1, NA // 2, NA)

        tile_x("c2a", 0, 1)

    both(z3, "c2g")
    sent("c0g")
    serve(12)
    z2("c1a", 0)

    @pl.when(r == 0)
    def _():
        tile_p("c0a", 0)

    serve(13)

    @pl.when(c == 0)
    def _():
        wait_mate(1, 0, NA // 2)

        @pl.when(r == 0)
        def _():
            tile_x("c2a", 0, 0)

    z3("c1a", 0)
    serve(14)

    @pl.when(c == 1)
    def _():
        z2("c2a", 0)

    @pl.when(r == 0)
    def _():
        z2("c0a", 0)

    serve(15)

    @pl.when(r == 1)
    def _():
        scale_a(1, 1)

    tile_b("c1a", 1)

    @pl.when(r == 1)
    def _():
        tile_p("c0a", 0)

        @pl.when(c == 0)
        def _():
            tile_x("c2a", 0, 0)

    @pl.when(c == 1)
    def _():
        @pl.when(r == 0)
        def _():
            wait_mate(1, NA // 2, NA)

        tile_x("c2a", 1, 1)
        z3("c2a", 0)

    z2("c1a", 1)

    @pl.when(r == 1)
    def _():
        z2("c0a", 0)

    for q in range(len(order) - LAG, len(order)):
        pass_far(q)
    tile_p("c0a", 1)

    @pl.when(c == 0)
    def _():
        z2("c2a", 0)

    z3("c0a", 0)

    @pl.when(c == 0)
    def _():
        wait_mate(1, NA // 2, NA)
        tile_x("c2a", 1, 0)
        z3("c2a", 0)

    z3("c1a", 1)
    z2("c0a", 1)
    z2("c2a", 1)
    z3("c0a", 1)
    z3("c2a", 1)

    def collect(kind, slot, stored):
        @pl.when(jnp.logical_not(stored))
        def _():
            for n in range(2):
                arrived(yr.at[kind, slot, n], y_recv.at[kind, slot, n])

    for kind in range(2):
        for slot in range(4):
            collect(kind, slot, slot == 2 * r + yh)
        for h in range(2):
            collect(kind, 8 + h, h == yh)
            collect(kind, 4 + h, jnp.logical_and(h == yh, 2 * r + c != 2))
            collect(kind, 6 + h, c == 1)

    def product(index, slots):
        @pl.loop(0, 3)
        def _(k):
            rows = pl.ds(pl.multiple_of(k * 32, 32), 32)
            for n in range(2):
                grams = []
                for kind in range(2):
                    gram = decode(yr[kind, slots[0], n, rows])
                    for slot in slots[1:]:
                        gram += decode(yr[kind, slot, n, rows])
                    grams.append(gram)
                out[index, rows, WIDE * n : WIDE * n + WIDE] = grams[0] * grams[1]

    product(0, (8, 9))
    product(2, (0, 1, 2, 3))

    @pl.when(c == 0)
    def _():
        product(1, (4, 5, 6, 7))

    @pl.when(c == 1)
    def _():
        product(1, (4, 5))

    for kind in (0, 1):
        @pl.loop(0, kinds[kind][5])
        def _(k):
            x_copy(kind, k, False).wait_send()
            c_copy(kind, k, 1).wait_send()

    @pl.when(c == 0)
    def _():
        for copy in w_copies():
            copy.wait_send()

    for step_ in range(1, 8):
        sum_copy(step_).wait_send()
    for copy in near:
        copy.wait_send()

    @pl.when(r == 1)
    def _():
        for copy in inv_far():
            copy.wait_send()

    @pl.when(c == 1)
    def _():
        sent("wg")
        sent("wa")

    for unit in ("c1g", "c2g", "c0a", "c1a", "c2a"):
        sent(unit)


def on_device(acts, grads):
    dma = pltpu.SemaphoreType.DMA
    n = len(UNITS)
    slots = 7
    any_space = pl.BlockSpec(memory_space=pl.ANY)
    result = pl.pallas_call(
        kernel,
        out_shape=(
            jax.ShapeDtypeStruct((3, SEG, ROWS), F32),
            jax.ShapeDtypeStruct((ROWS, KA), BF16),
            jax.ShapeDtypeStruct((ROWS, KG), BF16),
        ),
        in_specs=[any_space, any_space],
        out_specs=(pl.BlockSpec(memory_space=pltpu.VMEM), any_space, any_space),
        scratch_shapes=[
            pltpu.VMEM((ROWS, KA), BF16),
            pltpu.VMEM((ROWS, KG), BF16),
            pltpu.VMEM((4, ROWS, HA), BF16),
            pltpu.VMEM((4, ROWS, HG), BF16),
            pltpu.VMEM((WIDE, KA), BF16),
            pltpu.VMEM((slots, 8, SEG, ROWS), F32),
            pltpu.VMEM((slots, 2, 2, SEG, WIDE), BF16),
            pltpu.VMEM((slots, 2, 2, 2, SEG, WIDE), BF16),
            pltpu.VMEM((slots, 2, 2, SEG, WIDE), BF16),
            pltpu.VMEM((n, 2, 2, SEG, WIDE), BF16),
            pltpu.VMEM((n, 2, 2, 2, SEG, WIDE), BF16),
            pltpu.VMEM((2, 10, 2, SEG, WIDE), BF16),
            pltpu.VMEM((8, 8, ROWS), F32),
            pltpu.VMEM((6, 8, ROWS), F32),
            dma((2,)), dma((2,)), dma((NA,)), dma((NG,)), dma((NA,)), dma((NG,)),
            dma((NA,)), dma((NG,)), dma((NA,)), dma((NG,)),
            dma((NA,)), dma((NG,)), dma((NA,)), dma((NG,)),
            dma((2,)), dma((2,)), dma,
            dma((8,)), dma((8,)), dma((7,)), dma((6,)),
            dma((n, 2, 2)), dma((n, 2, 2)), dma((n, 2, 2)), dma((n, 2, 2)), dma((n, 2, 2)), dma((2, 10, 2)),
        ],
        compiler_params=pltpu.CompilerParams(
            collective_id=0, has_side_effects=True, vmem_limit_bytes=64 * 1024 * 1024 - 65536
        ),
        cost_estimate=pl.CostEstimate(
            flops=2 * 3 * ROWS * ROWS * (KA + KG), bytes_accessed=4 * ROWS * (KA + KG), transcendentals=0
        ),
    )(acts, grads)
    return jnp.transpose(result[0], (1, 0, 2))


def solution(mesh):
    placed = (P("ex", "tp"), P("ex", "tp"))
    return jax.shard_map(
        on_device,
        mesh=mesh,
        in_specs=placed,
        out_specs=P(("ex", "tp"), None, None),
        check_vma=False,
    )
```

```python
import functools

import jax
import jax.numpy as jnp
from jax import lax
from jax.experimental import pallas as pl
from jax.experimental.pallas import tpu as pltpu
from jax.sharding import PartitionSpec as P

epsilon = 1e-06
MESH = pl.DeviceIdType.MESH
F32 = jnp.float32
BF16 = jnp.bfloat16

ROWS = 768
SEG = 96
KA, KG = 3584, 1024
HA, HG = KA // 2, KG // 2
NA, NG = 4, 1
CA, CG = ROWS // NA, ROWS // NG
WIDE = ROWS // 2

SCALE, SHIFT = 248.0, 124.0

UNITS = ["dg", "da", "wg", "wa", "c0g", "c1g", "c2g", "c0a", "c1a", "c2a"]
U = {name: i for i, name in enumerate(UNITS)}
SLOT = dict(dg=0, da=1, wg=2, wa=3, c0g=4, c1g=5, c2g=6, c0a=7, c1a=1, c2a=0)


def encode(value):
    power = jnp.exp2(jnp.abs(value) * SCALE - SHIFT)
    return jnp.where(value < 0, -power, power).astype(BF16)


def decode(code):
    wide = code.astype(F32)
    size = jnp.log(jnp.abs(wide)) * (1.4426950408889634 / SCALE) + SHIFT / SCALE
    return jnp.where(wide < 0, -size, size)


def dot_rows(left, right):
    return lax.dot_general(
        left, right, (((1,), (1,)), ((), ())), preferred_element_type=F32
    )


def kernel(
    acts, grads, out, w_a, w_g,
    own_a, own_g, u_a, u_g, tmp, part, z1s, z2s, ys, z1r, z2r, yr, sums, inv,
    own_sem, keep_sem, pair_send_a, pair_send_g, ab_a, ab_g, x_send_a, x_send_g, x_recv_a, x_recv_g,
    c_send_a, c_send_g, c_recv_a, c_recv_g, w_send, w_recv, w_load,
    sum_send, sum_recv, inv_send, inv_recv,
    z1_send, z1_recv, z2_send, z2_recv, y_send, y_recv,
):
    ex, tp = lax.axis_index("ex"), lax.axis_index("tp")
    x, r, c = ex // 4, (ex // 2) % 2, ex % 2
    yh, z = tp // 4, tp % 4
    x_next, x_prev = (x + 1) % 4, (x + 3) % 4
    z_next, z_prev, z_far = (z + 1) % 4, (z + 3) % 4, (z + 2) % 4

    def dev(xx, rr, cc, hh=yh, zz=z):
        return (xx * 4 + rr * 2 + cc, hh * 4 + zz)

    def remote(src, dst, send, recv, device):
        return pltpu.make_async_remote_copy(
            src_ref=src, dst_ref=dst, send_sem=send, recv_sem=recv,
            device_id=device, device_id_type=MESH,
        )

    def arrived(ref, sem):
        pltpu.make_async_copy(ref, ref, sem).wait()

    pltpu.make_async_copy(acts, own_a, own_sem.at[0]).start()
    pltpu.make_async_copy(grads, own_g, own_sem.at[1]).start()

    barrier = pltpu.get_barrier_semaphore()

    def greet(device):
        pl.semaphore_signal(barrier, inc=1, device_id=device, device_id_type=MESH)

    for step in range(1, 8):
        greet((ex, (tp + step) % 8))
    for rr, cc in ((0, 1), (1, 0), (1, 1)):
        greet(dev(x, (r + rr) % 2, (c + cc) % 2))
        greet(dev(x, (r + rr) % 2, (c + cc) % 2, 1 - yh))
    for cc in range(2):
        for hh in range(2):
            greet(dev(x_prev, r, cc, hh))
            greet(dev(x_next, r, cc, hh))
    pl.semaphore_wait(barrier, 21)

    pair, mate = dev(x, 1 - r, c), dev(x, r, 1 - c)
    aside = dev((x + 3 + 2 * r) % 4, r, c)
    col_a = pl.multiple_of(r * HA, 128), pl.multiple_of((1 - r) * HA, 128)
    col_g = pl.multiple_of(r * HG, 128), pl.multiple_of((1 - r) * HG, 128)

    kinds = {
        0: (grads, u_g, col_g, HG, CG, NG, pair_send_g, ab_g, x_send_g, x_recv_g, c_send_g, c_recv_g),
        1: (acts, u_a, col_a, HA, CA, NA, pair_send_a, ab_a, x_send_a, x_recv_a, c_send_a, c_recv_a),
    }

    def rows_of(kind, k):
        chunk = kinds[kind][4]
        return pl.ds(k * chunk if isinstance(k, int) else pl.multiple_of(k * chunk, chunk), chunk)

    def pair_copy(kind, k):
        src, slots, cols, half, _, _, send, recv = kinds[kind][:8]
        rows = rows_of(kind, k)
        return remote(src.at[rows, pl.ds(cols[1], half)], slots.at[r, rows], send.at[k], recv.at[k], pair)

    def keep_copy(kind):
        src, slots, cols, half = kinds[kind][:4]
        return pltpu.make_async_copy(src.at[:, pl.ds(cols[0], half)], slots.at[r], keep_sem.at[kind])

    def x_copy(kind, k):
        src, slots, cols, half = kinds[kind][:4]
        send, recv = kinds[kind][8:10]
        rows = rows_of(kind, k)
        return remote(src.at[rows, pl.ds(cols[0], half)], slots.at[2, rows], send.at[k], recv.at[k], aside)

    def c_copy(kind, k, which):
        src, slots, cols, half = kinds[kind][:4]
        send, recv = kinds[kind][10:12]
        rows = rows_of(kind, k)
        source = src.at[rows, pl.ds(cols[0], half)] if which == 0 else slots.at[which, rows]
        return remote(source, slots.at[3, rows], send.at[k], recv.at[k], mate)

    def launch(kind, k):
        pair_copy(kind, k).start()
        x_copy(kind, k).start()

    launch(0, 0)
    for kind in (0, 1):
        keep_copy(kind).start()

        @pl.when(jnp.logical_and(r == 1, c == 0))
        def _():
            for k in range(kinds[kind][5]):
                c_copy(kind, k, 0).start()

    def w_copies():
        return (
            remote(own_a, w_a, w_send.at[0], w_recv.at[0], mate),
            remote(own_g, w_g, w_send.at[1], w_recv.at[1], mate),
        )

    def land(kind, k):
        slots, pair_recv, x_recv = kinds[kind][1], kinds[kind][7], kinds[kind][9]
        rows = rows_of(kind, k)
        arrived(slots.at[1 - r, rows], pair_recv.at[k])

        @pl.when(r == 0)
        def _():
            c_copy(kind, k, 1).start()

        arrived(slots.at[2, rows], x_recv.at[k])

        @pl.when(jnp.logical_and(r == 1, c == 1))
        def _():
            c_copy(kind, k, 2).start()

    def wait_gone(kind, first, last):
        for k in range(first, last):
            c_copy(kind, k, 1).wait_send()

    def wait_mate(kind, first, last):
        slots, recv = kinds[kind][1], kinds[kind][11]
        for k in range(first, last):
            arrived(slots.at[3, rows_of(kind, k)], recv.at[k])

    def put_sums(ref, row, width):
        @pl.loop(0, ROWS // 128)
        def _(i):
            rows = pl.ds(pl.multiple_of(i * 128, 128), 128)
            total = jnp.zeros((128, 128), F32)
            for j in range(width // 128):
                value = ref[rows, 128 * j : 128 * j + 128].astype(F32)
                total += value * value
            sums[tp, row : row + 1, rows] = jnp.sum(total.T, axis=0, keepdims=True)

    sums[tp] = jnp.zeros((8, ROWS), F32)
    arrived(own_g, own_sem.at[1])
    put_sums(own_g, 0, KG)
    arrived(own_a, own_sem.at[0])
    put_sums(own_a, 1, KA)

    def sum_copy(step):
        peer = (tp + step) % 8
        return remote(sums.at[tp], sums.at[tp], sum_send.at[step], sum_recv.at[tp], (ex, peer))

    for step in range(1, 8):
        sum_copy(step).start()
    for step in range(1, 8):
        source = (tp + step) % 8
        arrived(sums.at[source], sum_recv.at[source])
    total = sums[0]
    for i in range(1, 8):
        total += sums[i]
    mine = 2 * r + c
    inv[mine] = 1.0 / jnp.sqrt(total + epsilon)

    def inv_near():
        return [
            remote(inv.at[mine], inv.at[mine], inv_send.at[i], inv_recv.at[mine],
                   dev(x, (r + rr) % 2, (c + cc) % 2))
            for i, (rr, cc) in enumerate(((0, 1), (1, 0), (1, 1)))
        ]
    def inv_far():
        return [
            remote(inv.at[mine], inv.at[4 + c], inv_send.at[3], inv_recv.at[4 + c],
                   dev((x + 3 + 2 * r) % 4, r, c)),
            remote(inv.at[mine], inv.at[4 + c], inv_send.at[4], inv_recv.at[4 + c],
                   dev((x + 3 + 2 * r) % 4, r, 1 - c)),
        ]

    near = inv_near()
    for copy in near + inv_far():
        copy.start()

    def scale_rows(src, dst, block, row, start, count, width):
        @pl.loop(0, count // 128)
        def _(i):
            rows = pl.ds(pl.multiple_of(i * 128, 128), 128)
            lanes = pl.ds(pl.multiple_of(start + i * 128, 128), 128)
            col = jnp.broadcast_to(inv[block, row : row + 1, lanes], (128, 128)).T
            for j in range(width // 128):
                cols = slice(128 * j, 128 * j + 128)
                dst[rows, cols] = (src[rows, cols].astype(F32) * col).astype(BF16)

    def by_rows(unit):
        if unit[:2] == "c1":
            return 1 - r
        if unit[:2] == "c2":
            return 1 - r * c
        return int(unit[0] != "w")

    def quarter(unit, p):
        i, d = p // 2, p % 2
        flag = by_rows(unit)
        h = flag * i + (1 - flag) * d
        n = flag * d + (1 - flag) * i
        return h, pl.ds(n * WIDE if isinstance(n, int) else pl.multiple_of(n * WIDE, WIDE), WIDE), n

    z_peers = (ex, yh * 4 + z_next), (ex, yh * 4 + z_prev)
    bands = pl.ds(0, SEG // 2), pl.ds(SEG // 2, SEG // 2)

    def z1_copies(unit, p):
        u, s = U[unit], SLOT[unit]
        return [
            remote(z1s.at[s, p, bands[d]], z1r.at[u, p, bands[d]], z1_send.at[u, p, d], z1_recv.at[u, p, d], z_peers[d])
            for d in range(2)
        ]

    def z2_copies(unit, p):
        u, s = U[unit], SLOT[unit]
        return [
            remote(z2s.at[s, p, d], z2r.at[u, p, d], z2_send.at[u, p, d], z2_recv.at[u, p, d], z_peers[d])
            for d in range(2)
        ]

    def z1(unit, p):
        s = SLOT[unit]
        h, cols, _ = quarter(unit, p)
        z1s[s, p] = encode(part[s, h * 4 + z_far, :, cols])
        for copy in z1_copies(unit, p):
            copy.start()

    def z2(unit, p):
        u, s = U[unit], SLOT[unit]
        h, cols, _ = quarter(unit, p)
        for d in range(2):
            arrived(z1r.at[u, p, bands[d]], z1_recv.at[u, p, d])
        for way, to in ((0, z_next), (1, z_prev)):
            z2s[s, p, way, bands[way]] = encode(
                part[s, h * 4 + to, bands[way], cols] + decode(z1r[u, p, bands[way]])
            )
            z2s[s, p, way, bands[1 - way]] = encode(part[s, h * 4 + to, bands[1 - way], cols])
        for copy in z2_copies(unit, p):
            copy.start()

    def target(unit):
        if unit[0] == "d":
            return x, r, c, 8 + yh, yh == yh
        if unit[0] == "w":
            return x, r, c, 4 + yh, yh == yh
        source = r * 2 + yh
        if unit[:2] == "c0":
            return (x + 1 - r) % 4, 0, c, source, yh != yh
        if unit[:2] == "c1":
            return x, 1, c, source, r == 1
        return (x + (1 - c) * (1 - r)) % 4, c, 0, 4 + source, yh != yh

    def here(unit, p):
        return jnp.logical_and(target(unit)[4], yh == quarter(unit, p)[0])

    def y_copy(unit, p):
        u, s, kind = U[unit], SLOT[unit], int(unit[-1] == "a")
        xx, rr, cc, slot, _ = target(unit)
        h, _, n = quarter(unit, p)
        return remote(
            ys.at[s, p], yr.at[kind, slot, n], y_send.at[u, p], y_recv.at[kind, slot, n], dev(xx, rr, cc, h)
        )

    def z3(unit, p):
        u, s, kind = U[unit], SLOT[unit], int(unit[-1] == "a")
        h, cols, n = quarter(unit, p)
        slot = target(unit)[3]
        for d in range(2):
            arrived(z2r.at[u, p, d], z2_recv.at[u, p, d])
        total = part[s, h * 4 + z, :, cols] + decode(z2r[u, p, 0]) + decode(z2r[u, p, 1])
        ys[s, p] = encode(total)
        stays = here(unit, p)

        @pl.when(stays)
        def _():
            yr[kind, slot, n] = ys[s, p]

        @pl.when(jnp.logical_not(stays))
        def _():
            y_copy(unit, p).start()

    def gone(unit, p):
        for copy in z1_copies(unit, p) + z2_copies(unit, p):
            copy.wait_send()

        @pl.when(jnp.logical_not(here(unit, p)))
        def _():
            y_copy(unit, p).wait_send()

    def span(step, unit, first=0, last=4):
        @pl.loop(first, last)
        def _(p):
            step(unit, p)

    def every(step, *units):
        for unit in units:
            span(step, unit)

    def on_core(core, step, *units):
        @pl.when(c == core)
        def _():
            every(step, *units)

    def half_rows(i):
        return pl.ds(i * WIDE if isinstance(i, int) else pl.multiple_of(i * WIDE, WIDE), WIDE)

    def put(unit, p, left, right):
        h, cols, _ = quarter(unit, p)
        block = dot_rows(left, right)
        part[SLOT[unit], pl.ds(4 * h, 4), :, cols] = block.reshape(4, SEG, WIDE)

    scale_rows(own_g, own_g, mine, 0, 0, ROWS, KG)
    scale_rows(own_a, own_a, mine, 1, 0, ROWS, KA)

    @pl.when(c == 0)
    def _():
        for copy in w_copies():
            copy.start()

    def own_quarter(unit, p):
        ref = own_a if unit == "da" else own_g
        put(unit, p, ref[half_rows(p // 2), :], ref[half_rows(p % 2), :])
        z1(unit, p)

    span(own_quarter, "da", 0, 2)
    pair_copy(0, 0).wait_send()
    launch(1, 0)
    launch(1, 1)
    span(own_quarter, "da", 2, 4)
    span(own_quarter, "dg")

    spans = {0: (u_g, HG), 1: (u_a, HA)}
    block_3 = 2 * c + (1 - c) * (3 + 2 * r)

    def sides(unit):
        if unit[:2] == "c0":
            return 2 * (1 - r), 1 + r
        if unit[:2] == "c1":
            return 1, 0
        return 3 * c + 2 * (1 - c) * (1 - r), 3 * (1 - c)

    def tile(unit, p):
        slots, half = spans[int(unit[-1] == "a")]
        left, right = sides(unit)
        h, _, n = quarter(unit, p)
        put(unit, p, slots[left, half_rows(h), :], slots[right, half_rows(n), :])
        z1(unit, p)

    def scale(kind, slot, i):
        slots, half = spans[kind]
        block = slots.at[slot, half_rows(i)]
        number = block_3 if isinstance(slot, int) and slot == 3 else c + 2 * slot
        scale_rows(block, block, number, kind, i * WIDE, WIDE, half)

    for i in range(3):
        rr, cc = ((0, 1), (1, 0), (1, 1))[i]
        block = 2 * ((r + rr) % 2) + (c + cc) % 2
        arrived(inv.at[block], inv_recv.at[block])
    for block in (4, 5):
        arrived(inv.at[block], inv_recv.at[block])
    for kind in (0, 1):
        arrived(kinds[kind][1].at[r], keep_sem.at[kind])
    land(0, 0)
    wait_gone(0, 0, NG)
    wait_mate(0, 0, NG)
    for slot in (r, 1 - r, 2, 3):
        for i in range(2):
            scale(0, slot, i)
    every(tile, "c1g", "c0g", "c2g")
    every(z2, "da", "dg")

    @pl.when(c == 1)
    def _():
        arrived(w_a, w_recv.at[0])
        arrived(w_g, w_recv.at[1])

        @pl.loop(0, 2)
        def _(i):
            narrow = tmp.at[:, pl.ds(0, KG)]
            for unit, source, ref, own in (("wg", w_g, narrow, own_g), ("wa", w_a, tmp, own_a)):
                load = pltpu.make_async_copy(source.at[half_rows(i)], ref, w_load)
                load.start()
                load.wait()

                @pl.loop(0, 2)
                def _(d):
                    put(unit, 2 * i + d, own[half_rows(d), :], ref[...])
                    z1(unit, 2 * i + d)

    every(z2, "c1g", "c0g")
    for i in range(2):
        scale(1, r, i)
    every(z2, "c2g")
    pair_copy(1, 0).wait_send()
    launch(1, 2)
    on_core(1, z2, "wg", "wa")
    every(z3, "da", "dg")
    every(gone, "da", "dg")

    land(1, 0)
    land(1, 1)
    launch(1, 3)
    wait_gone(1, 0, NA // 2)
    scale(1, 1 - r, 0)
    span(tile, "c1a", 0, 2)
    scale(1, 2, 0)
    span(tile, "c0a", 0, 1)
    wait_mate(1, 0, NA // 2)
    scale(1, 3, 0)

    @pl.when(c == 0)
    def _():
        span(tile, "c2a", 0, 1)

    @pl.when(c == 1)
    def _():
        @pl.when(r == 1)
        def _():
            wait_mate(1, NA // 2, NA)
            scale(1, 3, 1)

        span(tile, "c2a", 0, 2)

    every(z3, "c1g", "c0g", "c2g")
    span(z2, "c1a", 0, 2)
    span(z2, "c0a", 0, 1)

    @pl.when(c == 0)
    def _():
        span(z2, "c2a", 0, 1)

    @pl.when(c == 1)
    def _():
        span(z2, "c2a", 0, 2)

    on_core(1, z3, "wg", "wa")
    span(z3, "c1a", 0, 2)
    span(z3, "c0a", 0, 1)
    span(z3, "c2a", 0, 1)

    @pl.when(c == 1)
    def _():
        span(z3, "c2a", 1, 2)

    land(1, 2)
    land(1, 3)

    @pl.when(r == 0)
    def _():
        wait_gone(1, NA // 2, NA)

    scale(1, 1 - r, 1)
    span(tile, "c1a", 2, 4)

    @pl.when(r == 1)
    def _():
        wait_gone(1, NA // 2, NA)

    scale(1, 2, 1)
    span(tile, "c0a", 1, 4)
    span(z2, "c1a", 2, 4)

    @pl.when(jnp.logical_not(jnp.logical_and(r == 1, c == 1)))
    def _():
        wait_mate(1, NA // 2, NA)
        scale(1, 3, 1)

    @pl.when(c == 0)
    def _():
        span(tile, "c2a", 1, 2)

    span(tile, "c2a", 2, 4)
    span(z2, "c0a", 1, 4)
    span(z3, "c1a", 2, 4)

    @pl.when(c == 0)
    def _():
        span(z2, "c2a", 1, 2)

    span(z2, "c2a", 2, 4)
    span(z3, "c0a", 1, 4)

    @pl.when(c == 0)
    def _():
        span(z3, "c2a", 1, 2)

    span(z3, "c2a", 2, 4)

    def collect(kind, slot, stored):
        @pl.when(jnp.logical_not(stored))
        def _():
            for n in range(2):
                arrived(yr.at[kind, slot, n], y_recv.at[kind, slot, n])

    for kind in range(2):
        for slot in range(4):
            collect(kind, slot, jnp.logical_and(r == 1, slot == 2 + yh))
        for h in range(2):
            collect(kind, 8 + h, h == yh)
            collect(kind, 4 + h, jnp.logical_and(h == yh, c == 1))
            collect(kind, 6 + h, c == 1)

    def product(index, slots):
        @pl.loop(0, 3)
        def _(k):
            rows = pl.ds(pl.multiple_of(k * 32, 32), 32)
            for n in range(2):
                grams = []
                for kind in range(2):
                    gram = decode(yr[kind, slots[0], n, rows])
                    for slot in slots[1:]:
                        gram += decode(yr[kind, slot, n, rows])
                    grams.append(gram)
                out[index, rows, WIDE * n : WIDE * n + WIDE] = grams[0] * grams[1]

    product(0, (8, 9))
    product(2, (0, 1, 2, 3))

    @pl.when(c == 0)
    def _():
        product(1, (4, 5, 6, 7))

    @pl.when(c == 1)
    def _():
        product(1, (4, 5))

    for kind in (0, 1):
        @pl.loop(0, kinds[kind][5])
        def _(k):
            x_copy(kind, k).wait_send()

    for k in range(1, NA):
        pair_copy(1, k).wait_send()

    @pl.when(c == 0)
    def _():
        for copy in w_copies():
            copy.wait_send()

    for step_ in range(1, 8):
        sum_copy(step_).wait_send()
    for copy in near + inv_far():
        copy.wait_send()

    on_core(1, gone, "wa", "wg")
    every(gone, "c0g", "c1g", "c2g", "c0a", "c1a", "c2a")


def on_device(acts, grads):
    dma = pltpu.SemaphoreType.DMA
    n = len(UNITS)
    slots = 8
    any_space = pl.BlockSpec(memory_space=pl.ANY)
    result = pl.pallas_call(
        kernel,
        out_shape=(
            jax.ShapeDtypeStruct((3, SEG, ROWS), F32),
            jax.ShapeDtypeStruct((ROWS, KA), BF16),
            jax.ShapeDtypeStruct((ROWS, KG), BF16),
        ),
        in_specs=[any_space, any_space],
        out_specs=(pl.BlockSpec(memory_space=pltpu.VMEM), any_space, any_space),
        scratch_shapes=[
            pltpu.VMEM((ROWS, KA), BF16),
            pltpu.VMEM((ROWS, KG), BF16),
            pltpu.VMEM((4, ROWS, HA), BF16),
            pltpu.VMEM((4, ROWS, HG), BF16),
            pltpu.VMEM((WIDE, KA), BF16),
            pltpu.VMEM((slots, 8, SEG, ROWS), F32),
            pltpu.VMEM((slots, 4, SEG, WIDE), BF16),
            pltpu.VMEM((slots, 4, 2, SEG, WIDE), BF16),
            pltpu.VMEM((slots, 4, SEG, WIDE), BF16),
            pltpu.VMEM((n, 4, SEG, WIDE), BF16),
            pltpu.VMEM((n, 4, 2, SEG, WIDE), BF16),
            pltpu.VMEM((2, 10, 2, SEG, WIDE), BF16),
            pltpu.VMEM((8, 8, ROWS), F32),
            pltpu.VMEM((6, 8, ROWS), F32),
            dma((2,)), dma((2,)), dma((NA,)), dma((NG,)), dma((NA,)), dma((NG,)),
            dma((NA,)), dma((NG,)), dma((NA,)), dma((NG,)),
            dma((NA,)), dma((NG,)), dma((NA,)), dma((NG,)),
            dma((2,)), dma((2,)), dma,
            dma((8,)), dma((8,)), dma((5,)), dma((6,)),
            dma((n, 4, 2)), dma((n, 4, 2)), dma((n, 4, 2)), dma((n, 4, 2)), dma((n, 4)), dma((2, 10, 2)),
        ],
        compiler_params=pltpu.CompilerParams(
            collective_id=0, has_side_effects=True, vmem_limit_bytes=64 * 1024 * 1024 - 65536
        ),
        cost_estimate=pl.CostEstimate(
            flops=2 * 3 * ROWS * ROWS * (KA + KG), bytes_accessed=4 * ROWS * (KA + KG), transcendentals=0
        ),
    )(acts, grads)
    return jnp.transpose(result[0], (1, 0, 2))


def solution(mesh):
    placed = (P("ex", "tp"), P("ex", "tp"))
    return jax.shard_map(
        on_device,
        mesh=mesh,
        in_specs=placed,
        out_specs=P(("ex", "tp"), None, None),
        check_vma=False,
    )
```

```python
import functools

import jax
import jax.numpy as jnp
from jax import lax
from jax.experimental import pallas as pl
from jax.experimental.pallas import tpu as pltpu
from jax.sharding import PartitionSpec as P

epsilon = 1e-06
MESH = pl.DeviceIdType.MESH
F32 = jnp.float32
BF16 = jnp.bfloat16

ROWS = 768
SEG = 96
KA, KG = 3584, 1024
HA, HG = KA // 2, KG // 2
NA, NG = 4, 1
CA, CG = ROWS // NA, ROWS // NG
WIDE = ROWS // 2

SCALE, SHIFT = 248.0, 124.0

UNITS = ["dg", "da", "wg", "wa", "c0g", "c1g", "c2g", "c0a", "c1a", "c2a"]
U = {name: i for i, name in enumerate(UNITS)}
SLOT = dict(dg=0, da=1, wg=2, wa=3, c0g=4, c1g=5, c2g=6, c0a=7, c1a=1, c2a=0)


def encode(value):
    power = jnp.exp2(jnp.abs(value) * SCALE - SHIFT)
    return jnp.where(value < 0, -power, power).astype(BF16)


def decode(code):
    wide = code.astype(F32)
    size = jnp.log(jnp.abs(wide)) * (1.4426950408889634 / SCALE) + SHIFT / SCALE
    return jnp.where(wide < 0, -size, size)


def dot_rows(left, right):
    return lax.dot_general(
        left, right, (((1,), (1,)), ((), ())), preferred_element_type=F32
    )


def kernel(
    acts, grads, out, w_a, w_g,
    own_a, own_g, u_a, u_g, tmp, part, z1s, z2s, ys, z1r, z2r, yr, sums, inv,
    own_sem, keep_sem, pair_send_a, pair_send_g, ab_a, ab_g, x_send_a, x_send_g, x_recv_a, x_recv_g,
    c_send_a, c_send_g, c_recv_a, c_recv_g, w_send, w_recv, w_load,
    sum_send, sum_recv, inv_send, inv_recv,
    z1_send, z1_recv, z2_send, z2_recv, y_send, y_recv,
):
    ex, tp = lax.axis_index("ex"), lax.axis_index("tp")
    x, r, c = ex // 4, (ex // 2) % 2, ex % 2
    yh, z = tp // 4, tp % 4
    x_next, x_prev = (x + 1) % 4, (x + 3) % 4
    z_next, z_prev, z_far = (z + 1) % 4, (z + 3) % 4, (z + 2) % 4

    def dev(xx, rr, cc, hh=yh, zz=z):
        return (xx * 4 + rr * 2 + cc, hh * 4 + zz)

    def remote(src, dst, send, recv, device):
        return pltpu.make_async_remote_copy(
            src_ref=src, dst_ref=dst, send_sem=send, recv_sem=recv,
            device_id=device, device_id_type=MESH,
        )

    def arrived(ref, sem):
        pltpu.make_async_copy(ref, ref, sem).wait()

    pltpu.make_async_copy(acts, own_a, own_sem.at[0]).start()
    pltpu.make_async_copy(grads, own_g, own_sem.at[1]).start()

    barrier = pltpu.get_barrier_semaphore()

    def greet(device):
        pl.semaphore_signal(barrier, inc=1, device_id=device, device_id_type=MESH)

    for step in range(1, 8):
        greet((ex, (tp + step) % 8))
    for rr, cc in ((0, 1), (1, 0), (1, 1)):
        greet(dev(x, (r + rr) % 2, (c + cc) % 2))
        greet(dev(x, (r + rr) % 2, (c + cc) % 2, 1 - yh))
    for cc in range(2):
        for hh in range(2):
            greet(dev(x_prev, r, cc, hh))
            greet(dev(x_next, r, cc, hh))
    pl.semaphore_wait(barrier, 21)

    pair, mate = dev(x, 1 - r, c), dev(x, r, 1 - c)
    aside = dev((x + 3 + 2 * r) % 4, r, c)
    col_a = pl.multiple_of(r * HA, 128), pl.multiple_of((1 - r) * HA, 128)
    col_g = pl.multiple_of(r * HG, 128), pl.multiple_of((1 - r) * HG, 128)

    kinds = {
        0: (grads, u_g, col_g, HG, CG, NG, pair_send_g, ab_g, x_send_g, x_recv_g, c_send_g, c_recv_g),
        1: (acts, u_a, col_a, HA, CA, NA, pair_send_a, ab_a, x_send_a, x_recv_a, c_send_a, c_recv_a),
    }

    def rows_of(kind, k):
        chunk = kinds[kind][4]
        return pl.ds(k * chunk if isinstance(k, int) else pl.multiple_of(k * chunk, chunk), chunk)

    def pair_copy(kind, k):
        src, slots, cols, half, _, _, send, recv = kinds[kind][:8]
        rows = rows_of(kind, k)
        return remote(src.at[rows, pl.ds(cols[1], half)], slots.at[r, rows], send.at[k], recv.at[k], pair)

    def keep_copy(kind):
        src, slots, cols, half = kinds[kind][:4]
        return pltpu.make_async_copy(src.at[:, pl.ds(cols[0], half)], slots.at[r], keep_sem.at[kind])

    def x_copy(kind, k):
        src, slots, cols, half = kinds[kind][:4]
        send, recv = kinds[kind][8:10]
        rows = rows_of(kind, k)
        return remote(src.at[rows, pl.ds(cols[0], half)], slots.at[2, rows], send.at[k], recv.at[k], aside)

    def c_copy(kind, k, which):
        src, slots, cols, half = kinds[kind][:4]
        send, recv = kinds[kind][10:12]
        rows = rows_of(kind, k)
        source = src.at[rows, pl.ds(cols[0], half)] if which == 0 else slots.at[which, rows]
        return remote(source, slots.at[3, rows], send.at[k], recv.at[k], mate)

    def launch(kind, k):
        pair_copy(kind, k).start()
        x_copy(kind, k).start()

    launch(0, 0)
    for kind in (0, 1):
        keep_copy(kind).start()

        @pl.when(jnp.logical_and(r == 1, c == 0))
        def _():
            for k in range(kinds[kind][5]):
                c_copy(kind, k, 0).start()

    def w_copies():
        return (
            remote(own_a, w_a, w_send.at[0], w_recv.at[0], mate),
            remote(own_g, w_g, w_send.at[1], w_recv.at[1], mate),
        )

    def land(kind, k):
        slots, pair_recv, x_recv = kinds[kind][1], kinds[kind][7], kinds[kind][9]
        rows = rows_of(kind, k)
        arrived(slots.at[1 - r, rows], pair_recv.at[k])

        @pl.when(r == 0)
        def _():
            c_copy(kind, k, 1).start()

        arrived(slots.at[2, rows], x_recv.at[k])

        @pl.when(jnp.logical_and(r == 1, c == 1))
        def _():
            c_copy(kind, k, 2).start()

    def wait_gone(kind, first, last):
        for k in range(first, last):
            c_copy(kind, k, 1).wait_send()

    def wait_mate(kind, first, last):
        slots, recv = kinds[kind][1], kinds[kind][11]
        for k in range(first, last):
            arrived(slots.at[3, rows_of(kind, k)], recv.at[k])

    def put_sums(ref, row, width):
        @pl.loop(0, ROWS // 128)
        def _(i):
            rows = pl.ds(pl.multiple_of(i * 128, 128), 128)
            total = jnp.zeros((128, 128), F32)
            for j in range(width // 128):
                value = ref[rows, 128 * j : 128 * j + 128].astype(F32)
                total += value * value
            sums[tp, row : row + 1, rows] = jnp.sum(total.T, axis=0, keepdims=True)

    sums[tp] = jnp.zeros((8, ROWS), F32)
    arrived(own_g, own_sem.at[1])
    put_sums(own_g, 0, KG)
    arrived(own_a, own_sem.at[0])
    put_sums(own_a, 1, KA)

    def sum_copy(step):
        peer = (tp + step) % 8
        return remote(sums.at[tp], sums.at[tp], sum_send.at[step], sum_recv.at[tp], (ex, peer))

    for step in range(1, 8):
        sum_copy(step).start()
    for step in range(1, 8):
        source = (tp + step) % 8
        arrived(sums.at[source], sum_recv.at[source])
    total = sums[0]
    for i in range(1, 8):
        total += sums[i]
    mine = 2 * r + c
    inv[mine] = 1.0 / jnp.sqrt(total + epsilon)

    def inv_near():
        return [
            remote(inv.at[mine], inv.at[mine], inv_send.at[i], inv_recv.at[mine],
                   dev(x, (r + rr) % 2, (c + cc) % 2))
            for i, (rr, cc) in enumerate(((0, 1), (1, 0), (1, 1)))
        ]
    def inv_far():
        return [
            remote(inv.at[mine], inv.at[4 + c], inv_send.at[3], inv_recv.at[4 + c],
                   dev((x + 3 + 2 * r) % 4, r, c)),
            remote(inv.at[mine], inv.at[4 + c], inv_send.at[4], inv_recv.at[4 + c],
                   dev((x + 3 + 2 * r) % 4, r, 1 - c)),
        ]

    near = inv_near()
    for copy in near + inv_far():
        copy.start()

    def scale_rows(src, dst, block, row, start, count, width):
        @pl.loop(0, count // 128)
        def _(i):
            rows = pl.ds(pl.multiple_of(i * 128, 128), 128)
            lanes = pl.ds(pl.multiple_of(start + i * 128, 128), 128)
            col = jnp.broadcast_to(inv[block, row : row + 1, lanes], (128, 128)).T
            for j in range(width // 128):
                cols = slice(128 * j, 128 * j + 128)
                dst[rows, cols] = (src[rows, cols].astype(F32) * col).astype(BF16)

    def by_rows(unit):
        if unit[:2] == "c1":
            return 1 - r
        if unit[:2] == "c2":
            return 1 - r * c
        return int(unit[0] != "w")

    def quarter(unit, p):
        i, d = p // 2, p % 2
        flag = by_rows(unit)
        h = flag * i + (1 - flag) * d
        n = flag * d + (1 - flag) * i
        return h, pl.ds(n * WIDE if isinstance(n, int) else pl.multiple_of(n * WIDE, WIDE), WIDE), n

    z_peers = (ex, yh * 4 + z_next), (ex, yh * 4 + z_prev)
    bands = pl.ds(0, SEG // 2), pl.ds(SEG // 2, SEG // 2)

    def z1_copies(unit, p):
        u, s = U[unit], SLOT[unit]
        return [
            remote(z1s.at[s, p, bands[d]], z1r.at[u, p, bands[d]], z1_send.at[u, p, d], z1_recv.at[u, p, d], z_peers[d])
            for d in range(2)
        ]

    def z2_copies(unit, p):
        u, s = U[unit], SLOT[unit]
        return [
            remote(z2s.at[s, p, d], z2r.at[u, p, d], z2_send.at[u, p, d], z2_recv.at[u, p, d], z_peers[d])
            for d in range(2)
        ]

    def z1(unit, p):
        s = SLOT[unit]
        h, cols, _ = quarter(unit, p)
        z1s[s, p] = encode(part[s, h * 4 + z_far, :, cols])
        for copy in z1_copies(unit, p):
            copy.start()

    def z2(unit, p):
        u, s = U[unit], SLOT[unit]
        h, cols, _ = quarter(unit, p)
        for d in range(2):
            arrived(z1r.at[u, p, bands[d]], z1_recv.at[u, p, d])
        for way, to in ((0, z_next), (1, z_prev)):
            z2s[s, p, way, bands[way]] = encode(
                part[s, h * 4 + to, bands[way], cols] + decode(z1r[u, p, bands[way]])
            )
            z2s[s, p, way, bands[1 - way]] = encode(part[s, h * 4 + to, bands[1 - way], cols])
        for copy in z2_copies(unit, p):
            copy.start()

    def target(unit):
        if unit[0] == "d":
            return x, r, c, 8 + yh, yh == yh
        if unit[0] == "w":
            return x, r, c, 4 + yh, yh == yh
        source = r * 2 + yh
        if unit[:2] == "c0":
            return (x + 1 - r) % 4, 0, c, source, yh != yh
        if unit[:2] == "c1":
            return x, 1, c, source, r == 1
        return (x + (1 - c) * (1 - r)) % 4, c, 0, 4 + source, yh != yh

    def here(unit, p):
        return jnp.logical_and(target(unit)[4], yh == quarter(unit, p)[0])

    def y_copy(unit, p):
        u, s, kind = U[unit], SLOT[unit], int(unit[-1] == "a")
        xx, rr, cc, slot, _ = target(unit)
        h, _, n = quarter(unit, p)
        return remote(
            ys.at[s, p], yr.at[kind, slot, n], y_send.at[u, p], y_recv.at[kind, slot, n], dev(xx, rr, cc, h)
        )

    def z3(unit, p):
        u, s, kind = U[unit], SLOT[unit], int(unit[-1] == "a")
        h, cols, n = quarter(unit, p)
        slot = target(unit)[3]
        for d in range(2):
            arrived(z2r.at[u, p, d], z2_recv.at[u, p, d])
        total = part[s, h * 4 + z, :, cols] + decode(z2r[u, p, 0]) + decode(z2r[u, p, 1])
        ys[s, p] = encode(total)
        stays = here(unit, p)

        @pl.when(stays)
        def _():
            yr[kind, slot, n] = ys[s, p]

        @pl.when(jnp.logical_not(stays))
        def _():
            y_copy(unit, p).start()

    def gone(unit, p):
        for copy in z1_copies(unit, p) + z2_copies(unit, p):
            copy.wait_send()

        @pl.when(jnp.logical_not(here(unit, p)))
        def _():
            y_copy(unit, p).wait_send()

    def span(step, unit, first=0, last=4):
        @pl.loop(first, last)
        def _(p):
            step(unit, p)

    def every(step, *units):
        for unit in units:
            span(step, unit)

    def on_core(core, step, *units):
        @pl.when(c == core)
        def _():
            every(step, *units)

    def half_rows(i):
        return pl.ds(i * WIDE if isinstance(i, int) else pl.multiple_of(i * WIDE, WIDE), WIDE)

    def put(unit, p, left, right):
        h, cols, _ = quarter(unit, p)
        block = dot_rows(left, right)
        part[SLOT[unit], pl.ds(4 * h, 4), :, cols] = block.reshape(4, SEG, WIDE)

    scale_rows(own_g, own_g, mine, 0, 0, ROWS, KG)
    scale_rows(own_a, own_a, mine, 1, 0, ROWS, KA)

    @pl.when(c == 0)
    def _():
        for copy in w_copies():
            copy.start()

    def own_quarter(unit, p):
        ref = own_a if unit == "da" else own_g
        put(unit, p, ref[half_rows(p // 2), :], ref[half_rows(p % 2), :])
        z1(unit, p)

    span(own_quarter, "da", 0, 2)
    pair_copy(0, 0).wait_send()
    launch(1, 0)
    launch(1, 1)
    span(own_quarter, "da", 2, 4)
    span(own_quarter, "dg")

    spans = {0: (u_g, HG), 1: (u_a, HA)}
    block_3 = 2 * c + (1 - c) * (3 + 2 * r)

    def sides(unit):
        if unit[:2] == "c0":
            return 2 * (1 - r), 1 + r
        if unit[:2] == "c1":
            return 1, 0
        return 3 * c + 2 * (1 - c) * (1 - r), 3 * (1 - c)

    def tile(unit, p):
        slots, half = spans[int(unit[-1] == "a")]
        left, right = sides(unit)
        h, _, n = quarter(unit, p)
        put(unit, p, slots[left, half_rows(h), :], slots[right, half_rows(n), :])
        z1(unit, p)

    def scale(kind, slot, i):
        slots, half = spans[kind]
        block = slots.at[slot, half_rows(i)]
        number = block_3 if isinstance(slot, int) and slot == 3 else c + 2 * slot
        scale_rows(block, block, number, kind, i * WIDE, WIDE, half)

    for i in range(3):
        rr, cc = ((0, 1), (1, 0), (1, 1))[i]
        block = 2 * ((r + rr) % 2) + (c + cc) % 2
        arrived(inv.at[block], inv_recv.at[block])
    for block in (4, 5):
        arrived(inv.at[block], inv_recv.at[block])
    for kind in (0, 1):
        arrived(kinds[kind][1].at[r], keep_sem.at[kind])
    land(0, 0)
    wait_gone(0, 0, NG)
    wait_mate(0, 0, NG)
    for slot in (r, 1 - r, 2, 3):
        for i in range(2):
            scale(0, slot, i)
    every(tile, "c1g", "c0g", "c2g")
    every(z2, "da", "dg")

    @pl.when(c == 1)
    def _():
        arrived(w_a, w_recv.at[0])
        arrived(w_g, w_recv.at[1])

        @pl.loop(0, 2)
        def _(i):
            narrow = tmp.at[:, pl.ds(0, KG)]
            for unit, source, ref, own in (("wg", w_g, narrow, own_g), ("wa", w_a, tmp, own_a)):
                load = pltpu.make_async_copy(source.at[half_rows(i)], ref, w_load)
                load.start()
                load.wait()

                @pl.loop(0, 2)
                def _(d):
                    put(unit, 2 * i + d, own[half_rows(d), :], ref[...])
                    z1(unit, 2 * i + d)

    every(z2, "c1g", "c0g")
    for i in range(2):
        scale(1, r, i)
    every(z2, "c2g")
    pair_copy(1, 0).wait_send()
    launch(1, 2)
    on_core(1, z2, "wg", "wa")
    every(z3, "da", "dg")
    every(gone, "da", "dg")

    land(1, 0)
    land(1, 1)
    launch(1, 3)
    wait_gone(1, 0, NA // 2)
    scale(1, 1 - r, 0)
    span(tile, "c1a", 0, 2)
    scale(1, 2, 0)
    span(tile, "c0a", 0, 1)
    wait_mate(1, 0, NA // 2)
    scale(1, 3, 0)

    @pl.when(c == 0)
    def _():
        span(tile, "c2a", 0, 1)

    @pl.when(c == 1)
    def _():
        @pl.when(r == 1)
        def _():
            wait_mate(1, NA // 2, NA)
            scale(1, 3, 1)

        span(tile, "c2a", 0, 2)

    every(z3, "c1g", "c0g", "c2g")
    span(z2, "c1a", 0, 2)
    span(z2, "c0a", 0, 1)

    @pl.when(c == 0)
    def _():
        span(z2, "c2a", 0, 1)

    @pl.when(c == 1)
    def _():
        span(z2, "c2a", 0, 2)

    on_core(1, z3, "wg", "wa")
    span(z3, "c1a", 0, 2)
    span(z3, "c0a", 0, 1)
    span(z3, "c2a", 0, 1)

    @pl.when(c == 1)
    def _():
        span(z3, "c2a", 1, 2)

    land(1, 2)
    land(1, 3)

    @pl.when(r == 0)
    def _():
        wait_gone(1, NA // 2, NA)

    scale(1, 1 - r, 1)
    span(tile, "c1a", 2, 4)

    @pl.when(r == 1)
    def _():
        wait_gone(1, NA // 2, NA)

    scale(1, 2, 1)
    span(tile, "c0a", 1, 4)
    span(z2, "c1a", 2, 4)

    @pl.when(jnp.logical_not(jnp.logical_and(r == 1, c == 1)))
    def _():
        wait_mate(1, NA // 2, NA)
        scale(1, 3, 1)

    @pl.when(c == 0)
    def _():
        span(tile, "c2a", 1, 2)

    span(tile, "c2a", 2, 4)
    span(z2, "c0a", 1, 4)
    span(z3, "c1a", 2, 4)

    @pl.when(c == 0)
    def _():
        span(z2, "c2a", 1, 2)

    span(z2, "c2a", 2, 4)

    def collect(kind, slot, stored):
        @pl.when(jnp.logical_not(stored))
        def _():
            for n in range(2):
                arrived(yr.at[kind, slot, n], y_recv.at[kind, slot, n])

    def gram_sum(kind, slots, n, rows):
        gram = decode(yr[kind, slots[0], n, rows])
        for slot in slots[1:]:
            gram += decode(yr[kind, slot, n, rows])
        return gram

    def fill(index, slots, kinds_in):
        @pl.loop(0, 3)
        def _(k):
            rows = pl.ds(pl.multiple_of(k * 32, 32), 32)
            for n in range(2):
                cols = slice(WIDE * n, WIDE * n + WIDE)
                value = gram_sum(kinds_in[0], slots, n, rows)
                if len(kinds_in) > 1:
                    value *= gram_sum(kinds_in[1], slots, n, rows)
                elif kinds_in[0] == 1:
                    value *= out[index, rows, cols]
                out[index, rows, cols] = value

    for kind in range(2):
        for h in range(2):
            collect(kind, 8 + h, h == yh)
    fill(0, (8, 9), (0, 1))
    for slot in range(4):
        collect(0, slot, jnp.logical_and(r == 1, slot == 2 + yh))
    fill(2, (0, 1, 2, 3), (0,))

    @pl.when(c == 0)
    def _():
        for slot in range(4, 8):
            collect(0, slot, yh != yh)
        fill(1, (4, 5, 6, 7), (0,))

    @pl.when(c == 1)
    def _():
        for kind in range(2):
            for h in range(2):
                collect(kind, 4 + h, h == yh)
        fill(1, (4, 5), (0, 1))

    span(z3, "c0a", 1, 4)

    @pl.when(c == 0)
    def _():
        span(z3, "c2a", 1, 2)

    span(z3, "c2a", 2, 4)

    for slot in range(4):
        collect(1, slot, jnp.logical_and(r == 1, slot == 2 + yh))
    fill(2, (0, 1, 2, 3), (1,))

    @pl.when(c == 0)
    def _():
        for slot in range(4, 8):
            collect(1, slot, yh != yh)
        fill(1, (4, 5, 6, 7), (1,))

    for kind in (0, 1):
        @pl.loop(0, kinds[kind][5])
        def _(k):
            x_copy(kind, k).wait_send()

    for k in range(1, NA):
        pair_copy(1, k).wait_send()

    @pl.when(c == 0)
    def _():
        for copy in w_copies():
            copy.wait_send()

    for step_ in range(1, 8):
        sum_copy(step_).wait_send()
    for copy in near + inv_far():
        copy.wait_send()

    on_core(1, gone, "wa", "wg")
    every(gone, "c0g", "c1g", "c2g", "c0a", "c1a", "c2a")


def on_device(acts, grads):
    dma = pltpu.SemaphoreType.DMA
    n = len(UNITS)
    slots = 8
    any_space = pl.BlockSpec(memory_space=pl.ANY)
    result = pl.pallas_call(
        kernel,
        out_shape=(
            jax.ShapeDtypeStruct((3, SEG, ROWS), F32),
            jax.ShapeDtypeStruct((ROWS, KA), BF16),
            jax.ShapeDtypeStruct((ROWS, KG), BF16),
        ),
        in_specs=[any_space, any_space],
        out_specs=(pl.BlockSpec(memory_space=pltpu.VMEM), any_space, any_space),
        scratch_shapes=[
            pltpu.VMEM((ROWS, KA), BF16),
            pltpu.VMEM((ROWS, KG), BF16),
            pltpu.VMEM((4, ROWS, HA), BF16),
            pltpu.VMEM((4, ROWS, HG), BF16),
            pltpu.VMEM((WIDE, KA), BF16),
            pltpu.VMEM((slots, 8, SEG, ROWS), F32),
            pltpu.VMEM((slots, 4, SEG, WIDE), BF16),
            pltpu.VMEM((slots, 4, 2, SEG, WIDE), BF16),
            pltpu.VMEM((slots, 4, SEG, WIDE), BF16),
            pltpu.VMEM((n, 4, SEG, WIDE), BF16),
            pltpu.VMEM((n, 4, 2, SEG, WIDE), BF16),
            pltpu.VMEM((2, 10, 2, SEG, WIDE), BF16),
            pltpu.VMEM((8, 8, ROWS), F32),
            pltpu.VMEM((6, 8, ROWS), F32),
            dma((2,)), dma((2,)), dma((NA,)), dma((NG,)), dma((NA,)), dma((NG,)),
            dma((NA,)), dma((NG,)), dma((NA,)), dma((NG,)),
            dma((NA,)), dma((NG,)), dma((NA,)), dma((NG,)),
            dma((2,)), dma((2,)), dma,
            dma((8,)), dma((8,)), dma((5,)), dma((6,)),
            dma((n, 4, 2)), dma((n, 4, 2)), dma((n, 4, 2)), dma((n, 4, 2)), dma((n, 4)), dma((2, 10, 2)),
        ],
        compiler_params=pltpu.CompilerParams(
            collective_id=0, has_side_effects=True, vmem_limit_bytes=64 * 1024 * 1024 - 65536
        ),
        cost_estimate=pl.CostEstimate(
            flops=2 * 3 * ROWS * ROWS * (KA + KG), bytes_accessed=4 * ROWS * (KA + KG), transcendentals=0
        ),
    )(acts, grads)
    return jnp.transpose(result[0], (1, 0, 2))


def solution(mesh):
    placed = (P("ex", "tp"), P("ex", "tp"))
    return jax.shard_map(
        on_device,
        mesh=mesh,
        in_specs=placed,
        out_specs=P(("ex", "tp"), None, None),
        check_vma=False,
    )
```

```python
import functools

import jax
import jax.numpy as jnp
from jax import lax
from jax.experimental import pallas as pl
from jax.experimental.pallas import tpu as pltpu
from jax.sharding import PartitionSpec as P

epsilon = 1e-06
MESH = pl.DeviceIdType.MESH
F32 = jnp.float32
BF16 = jnp.bfloat16

ROWS = 768
SEG = 96
KA, KG = 3584, 1024
HA, HG = KA // 2, KG // 2
NA, NG = 4, 1
CA, CG = ROWS // NA, ROWS // NG
WIDE = ROWS // 2

SCALE, SHIFT = 248.0, 124.0

UNITS = ["dg", "da", "wg", "wa", "c0g", "c1g", "c2g", "c0a", "c1a", "c2a"]
U = {name: i for i, name in enumerate(UNITS)}
SLOT = dict(dg=0, da=1, wg=2, wa=3, c0g=4, c1g=5, c2g=6, c0a=7, c1a=1, c2a=0)


def encode(value):
    power = jnp.exp2(jnp.abs(value) * SCALE - SHIFT)
    return jnp.where(value < 0, -power, power).astype(BF16)


def decode(code):
    wide = code.astype(F32)
    size = jnp.log(jnp.abs(wide)) * (1.4426950408889634 / SCALE) + SHIFT / SCALE
    return jnp.where(wide < 0, -size, size)


def dot_rows(left, right):
    return lax.dot_general(
        left, right, (((1,), (1,)), ((), ())), preferred_element_type=F32
    )


def kernel(
    acts, grads, out, w_a, w_g,
    own_a, own_g, u_a, u_g, tmp, part, z1s, z2s, ys, z1r, z2r, yr, sums, inv,
    own_sem, keep_sem, pair_send_a, pair_send_g, ab_a, ab_g, x_send_a, x_send_g, x_recv_a, x_recv_g,
    c_send_a, c_send_g, c_recv_a, c_recv_g, w_send, w_recv, w_load,
    sum_send, sum_recv, inv_send, inv_recv,
    z1_send, z1_recv, z2_send, z2_recv, y_send, y_recv,
):
    ex, tp = lax.axis_index("ex"), lax.axis_index("tp")
    x, r, c = ex // 4, (ex // 2) % 2, ex % 2
    yh, z = tp // 4, tp % 4
    x_next, x_prev = (x + 1) % 4, (x + 3) % 4
    z_next, z_prev, z_far = (z + 1) % 4, (z + 3) % 4, (z + 2) % 4

    def dev(xx, rr, cc, hh=yh, zz=z):
        return (xx * 4 + rr * 2 + cc, hh * 4 + zz)

    def remote(src, dst, send, recv, device):
        return pltpu.make_async_remote_copy(
            src_ref=src, dst_ref=dst, send_sem=send, recv_sem=recv,
            device_id=device, device_id_type=MESH,
        )

    def arrived(ref, sem):
        pltpu.make_async_copy(ref, ref, sem).wait()

    pltpu.make_async_copy(acts, own_a, own_sem.at[0]).start()
    pltpu.make_async_copy(grads, own_g, own_sem.at[1]).start()

    barrier = pltpu.get_barrier_semaphore()

    def greet(device):
        pl.semaphore_signal(barrier, inc=1, device_id=device, device_id_type=MESH)

    for step in range(1, 8):
        greet((ex, (tp + step) % 8))
    for rr, cc in ((0, 1), (1, 0), (1, 1)):
        greet(dev(x, (r + rr) % 2, (c + cc) % 2))
        greet(dev(x, (r + rr) % 2, (c + cc) % 2, 1 - yh))
    for cc in range(2):
        for hh in range(2):
            greet(dev(x_prev, r, cc, hh))
            greet(dev(x_next, r, cc, hh))
    pl.semaphore_wait(barrier, 21)

    pair, mate = dev(x, 1 - r, c), dev(x, r, 1 - c)
    aside = dev((x + 3 + 2 * r) % 4, r, c)
    col_a = pl.multiple_of(r * HA, 128), pl.multiple_of((1 - r) * HA, 128)
    col_g = pl.multiple_of(r * HG, 128), pl.multiple_of((1 - r) * HG, 128)

    kinds = {
        0: (grads, u_g, col_g, HG, CG, NG, pair_send_g, ab_g, x_send_g, x_recv_g, c_send_g, c_recv_g),
        1: (acts, u_a, col_a, HA, CA, NA, pair_send_a, ab_a, x_send_a, x_recv_a, c_send_a, c_recv_a),
    }

    def rows_of(kind, k):
        chunk = kinds[kind][4]
        return pl.ds(k * chunk if isinstance(k, int) else pl.multiple_of(k * chunk, chunk), chunk)

    def pair_copy(kind, k):
        src, slots, cols, half, _, _, send, recv = kinds[kind][:8]
        rows = rows_of(kind, k)
        return remote(src.at[rows, pl.ds(cols[1], half)], slots.at[r, rows], send.at[k], recv.at[k], pair)

    def keep_copy(kind):
        src, slots, cols, half = kinds[kind][:4]
        return pltpu.make_async_copy(src.at[:, pl.ds(cols[0], half)], slots.at[r], keep_sem.at[kind])

    def x_copy(kind, k):
        src, slots, cols, half = kinds[kind][:4]
        send, recv = kinds[kind][8:10]
        rows = rows_of(kind, k)
        return remote(src.at[rows, pl.ds(cols[0], half)], slots.at[2, rows], send.at[k], recv.at[k], aside)

    def c_copy(kind, k, which):
        src, slots, cols, half = kinds[kind][:4]
        send, recv = kinds[kind][10:12]
        rows = rows_of(kind, k)
        source = src.at[rows, pl.ds(cols[0], half)] if which == 0 else slots.at[which, rows]
        return remote(source, slots.at[3, rows], send.at[k], recv.at[k], mate)

    def launch(kind, k):
        pair_copy(kind, k).start()
        x_copy(kind, k).start()

    launch(0, 0)
    for kind in (0, 1):
        keep_copy(kind).start()

        @pl.when(jnp.logical_and(r == 1, c == 0))
        def _():
            for k in range(kinds[kind][5]):
                c_copy(kind, k, 0).start()

    def w_copies():
        return (
            remote(own_a, w_a, w_send.at[0], w_recv.at[0], mate),
            remote(own_g, w_g, w_send.at[1], w_recv.at[1], mate),
        )

    def land(kind, k):
        slots, pair_recv, x_recv = kinds[kind][1], kinds[kind][7], kinds[kind][9]
        rows = rows_of(kind, k)
        arrived(slots.at[1 - r, rows], pair_recv.at[k])

        @pl.when(r == 0)
        def _():
            c_copy(kind, k, 1).start()

        arrived(slots.at[2, rows], x_recv.at[k])

        @pl.when(jnp.logical_and(r == 1, c == 1))
        def _():
            c_copy(kind, k, 2).start()

    def wait_gone(kind, first, last):
        for k in range(first, last):
            c_copy(kind, k, 1).wait_send()

    def wait_mate(kind, first, last):
        slots, recv = kinds[kind][1], kinds[kind][11]
        for k in range(first, last):
            arrived(slots.at[3, rows_of(kind, k)], recv.at[k])

    def put_sums(ref, row, width):
        @pl.loop(0, ROWS // 128)
        def _(i):
            rows = pl.ds(pl.multiple_of(i * 128, 128), 128)
            total = jnp.zeros((128, 128), F32)
            for j in range(width // 128):
                value = ref[rows, 128 * j : 128 * j + 128].astype(F32)
                total += value * value
            sums[tp, row : row + 1, rows] = jnp.sum(total.T, axis=0, keepdims=True)

    sums[tp] = jnp.zeros((8, ROWS), F32)
    arrived(own_g, own_sem.at[1])
    put_sums(own_g, 0, KG)
    arrived(own_a, own_sem.at[0])
    put_sums(own_a, 1, KA)

    def sum_copy(step):
        peer = (tp + step) % 8
        return remote(sums.at[tp], sums.at[tp], sum_send.at[step], sum_recv.at[tp], (ex, peer))

    for step in range(1, 8):
        sum_copy(step).start()
    for step in range(1, 8):
        source = (tp + step) % 8
        arrived(sums.at[source], sum_recv.at[source])
    total = sums[0]
    for i in range(1, 8):
        total += sums[i]
    mine = 2 * r + c
    inv[mine] = 1.0 / jnp.sqrt(total + epsilon)

    def inv_near():
        return [
            remote(inv.at[mine], inv.at[mine], inv_send.at[i], inv_recv.at[mine],
                   dev(x, (r + rr) % 2, (c + cc) % 2))
            for i, (rr, cc) in enumerate(((0, 1), (1, 0), (1, 1)))
        ]
    def inv_far():
        return [
            remote(inv.at[mine], inv.at[4 + c], inv_send.at[3], inv_recv.at[4 + c],
                   dev((x + 3 + 2 * r) % 4, r, c)),
            remote(inv.at[mine], inv.at[4 + c], inv_send.at[4], inv_recv.at[4 + c],
                   dev((x + 3 + 2 * r) % 4, r, 1 - c)),
        ]

    near = inv_near()
    for copy in near + inv_far():
        copy.start()

    def scale_rows(src, dst, block, row, start, count, width):
        @pl.loop(0, count // 128)
        def _(i):
            rows = pl.ds(pl.multiple_of(i * 128, 128), 128)
            lanes = pl.ds(pl.multiple_of(start + i * 128, 128), 128)
            col = jnp.broadcast_to(inv[block, row : row + 1, lanes], (128, 128)).T
            for j in range(width // 128):
                cols = slice(128 * j, 128 * j + 128)
                dst[rows, cols] = (src[rows, cols].astype(F32) * col).astype(BF16)

    def by_rows(unit):
        if unit[:2] == "c1":
            return 1 - r
        if unit[:2] == "c2":
            return 1 - r * c
        return int(unit[0] != "w")

    def quarter(unit, p):
        i, d = p // 2, p % 2
        flag = by_rows(unit)
        h = flag * i + (1 - flag) * d
        n = flag * d + (1 - flag) * i
        return h, pl.ds(n * WIDE if isinstance(n, int) else pl.multiple_of(n * WIDE, WIDE), WIDE), n

    z_peers = (ex, yh * 4 + z_next), (ex, yh * 4 + z_prev)
    bands = pl.ds(0, SEG // 2), pl.ds(SEG // 2, SEG // 2)

    def z1_copies(unit, p):
        u, s = U[unit], SLOT[unit]
        return [
            remote(z1s.at[s, p, bands[d]], z1r.at[u, p, bands[d]], z1_send.at[u, p, d], z1_recv.at[u, p, d], z_peers[d])
            for d in range(2)
        ]

    def z2_copies(unit, p):
        u, s = U[unit], SLOT[unit]
        return [
            remote(z2s.at[s, p, d], z2r.at[u, p, d], z2_send.at[u, p, d], z2_recv.at[u, p, d], z_peers[d])
            for d in range(2)
        ]

    def z1(unit, p):
        s = SLOT[unit]
        h, cols, _ = quarter(unit, p)
        z1s[s, p] = encode(part[s, h * 4 + z_far, :, cols])
        for copy in z1_copies(unit, p):
            copy.start()

    def z2(unit, p):
        u, s = U[unit], SLOT[unit]
        h, cols, _ = quarter(unit, p)
        for d in range(2):
            arrived(z1r.at[u, p, bands[d]], z1_recv.at[u, p, d])
        for way, to in ((0, z_next), (1, z_prev)):
            z2s[s, p, way, bands[way]] = encode(
                part[s, h * 4 + to, bands[way], cols] + decode(z1r[u, p, bands[way]])
            )
            z2s[s, p, way, bands[1 - way]] = encode(part[s, h * 4 + to, bands[1 - way], cols])
        for copy in z2_copies(unit, p):
            copy.start()

    def target(unit):
        if unit[0] == "d":
            return x, r, c, 8 + yh, yh == yh
        if unit[0] == "w":
            return x, r, c, 4 + yh, yh == yh
        source = r * 2 + yh
        if unit[:2] == "c0":
            return (x + 1 - r) % 4, 0, c, source, yh != yh
        if unit[:2] == "c1":
            return x, 1, c, source, r == 1
        return (x + (1 - c) * (1 - r)) % 4, c, 0, 4 + source, yh != yh

    def here(unit, p):
        return jnp.logical_and(target(unit)[4], yh == quarter(unit, p)[0])

    def y_copy(unit, p):
        u, s, kind = U[unit], SLOT[unit], int(unit[-1] == "a")
        xx, rr, cc, slot, _ = target(unit)
        h, _, n = quarter(unit, p)
        return remote(
            ys.at[s, p], yr.at[kind, slot, n], y_send.at[u, p], y_recv.at[kind, slot, n], dev(xx, rr, cc, h)
        )

    def z3(unit, p):
        u, s, kind = U[unit], SLOT[unit], int(unit[-1] == "a")
        h, cols, n = quarter(unit, p)
        slot = target(unit)[3]
        for d in range(2):
            arrived(z2r.at[u, p, d], z2_recv.at[u, p, d])
        total = part[s, h * 4 + z, :, cols] + decode(z2r[u, p, 0]) + decode(z2r[u, p, 1])
        ys[s, p] = encode(total)
        stays = here(unit, p)

        @pl.when(stays)
        def _():
            yr[kind, slot, n] = ys[s, p]

        @pl.when(jnp.logical_not(stays))
        def _():
            y_copy(unit, p).start()

    def gone(unit, p):
        for copy in z1_copies(unit, p) + z2_copies(unit, p):
            copy.wait_send()

        @pl.when(jnp.logical_not(here(unit, p)))
        def _():
            y_copy(unit, p).wait_send()

    def span(step, unit, first=0, last=4):
        @pl.loop(first, last)
        def _(p):
            step(unit, p)

    def every(step, *units):
        for unit in units:
            span(step, unit)

    def on_core(core, step, *units):
        @pl.when(c == core)
        def _():
            every(step, *units)

    def half_rows(i):
        return pl.ds(i * WIDE if isinstance(i, int) else pl.multiple_of(i * WIDE, WIDE), WIDE)

    def put(unit, p, left, right):
        h, cols, _ = quarter(unit, p)
        block = dot_rows(left, right)
        part[SLOT[unit], pl.ds(4 * h, 4), :, cols] = block.reshape(4, SEG, WIDE)

    scale_rows(own_g, own_g, mine, 0, 0, ROWS, KG)
    scale_rows(own_a, own_a, mine, 1, 0, ROWS, KA)

    @pl.when(c == 0)
    def _():
        for copy in w_copies():
            copy.start()

    def own_quarter(unit, p):
        ref = own_a if unit == "da" else own_g
        put(unit, p, ref[half_rows(p // 2), :], ref[half_rows(p % 2), :])
        z1(unit, p)

    launch(1, 0)
    span(own_quarter, "da", 0, 2)
    pair_copy(0, 0).wait_send()
    launch(1, 1)
    span(own_quarter, "da", 2, 4)
    span(own_quarter, "dg")

    spans = {0: (u_g, HG), 1: (u_a, HA)}
    block_3 = 2 * c + (1 - c) * (3 + 2 * r)

    def sides(unit):
        if unit[:2] == "c0":
            return 2 * (1 - r), 1 + r
        if unit[:2] == "c1":
            return 1, 0
        return 3 * c + 2 * (1 - c) * (1 - r), 3 * (1 - c)

    def tile(unit, p):
        slots, half = spans[int(unit[-1] == "a")]
        left, right = sides(unit)
        h, _, n = quarter(unit, p)
        put(unit, p, slots[left, half_rows(h), :], slots[right, half_rows(n), :])
        z1(unit, p)

    def scale(kind, slot, i):
        slots, half = spans[kind]
        block = slots.at[slot, half_rows(i)]
        number = block_3 if isinstance(slot, int) and slot == 3 else c + 2 * slot
        scale_rows(block, block, number, kind, i * WIDE, WIDE, half)

    for i in range(3):
        rr, cc = ((0, 1), (1, 0), (1, 1))[i]
        block = 2 * ((r + rr) % 2) + (c + cc) % 2
        arrived(inv.at[block], inv_recv.at[block])
    for block in (4, 5):
        arrived(inv.at[block], inv_recv.at[block])
    for kind in (0, 1):
        arrived(kinds[kind][1].at[r], keep_sem.at[kind])
    land(0, 0)
    wait_gone(0, 0, NG)
    wait_mate(0, 0, NG)
    for slot in (r, 1 - r, 2, 3):
        for i in range(2):
            scale(0, slot, i)
    every(tile, "c1g", "c0g", "c2g")
    every(z2, "da", "dg")

    @pl.when(c == 1)
    def _():
        arrived(w_a, w_recv.at[0])
        arrived(w_g, w_recv.at[1])

        @pl.loop(0, 2)
        def _(i):
            narrow = tmp.at[:, pl.ds(0, KG)]
            for unit, source, ref, own in (("wg", w_g, narrow, own_g), ("wa", w_a, tmp, own_a)):
                load = pltpu.make_async_copy(source.at[half_rows(i)], ref, w_load)
                load.start()
                load.wait()

                @pl.loop(0, 2)
                def _(d):
                    put(unit, 2 * i + d, own[half_rows(d), :], ref[...])
                    z1(unit, 2 * i + d)

    every(z2, "c1g", "c0g")
    for i in range(2):
        scale(1, r, i)
    every(z2, "c2g")
    pair_copy(1, 0).wait_send()
    launch(1, 2)
    on_core(1, z2, "wg", "wa")
    every(z3, "da", "dg")
    every(gone, "da", "dg")

    land(1, 0)
    land(1, 1)
    launch(1, 3)
    wait_gone(1, 0, NA // 2)
    scale(1, 1 - r, 0)
    span(tile, "c1a", 0, 2)
    scale(1, 2, 0)
    span(tile, "c0a", 0, 1)
    wait_mate(1, 0, NA // 2)
    scale(1, 3, 0)

    @pl.when(c == 0)
    def _():
        span(tile, "c2a", 0, 1)

    @pl.when(c == 1)
    def _():
        @pl.when(r == 1)
        def _():
            wait_mate(1, NA // 2, NA)
            scale(1, 3, 1)

        span(tile, "c2a", 0, 2)

    every(z3, "c1g", "c0g", "c2g")
    span(z2, "c1a", 0, 2)
    span(z2, "c0a", 0, 1)

    @pl.when(c == 0)
    def _():
        span(z2, "c2a", 0, 1)

    @pl.when(c == 1)
    def _():
        span(z2, "c2a", 0, 2)

    on_core(1, z3, "wg", "wa")
    span(z3, "c1a", 0, 2)
    span(z3, "c0a", 0, 1)
    span(z3, "c2a", 0, 1)

    @pl.when(c == 1)
    def _():
        span(z3, "c2a", 1, 2)

    land(1, 2)
    land(1, 3)

    @pl.when(r == 0)
    def _():
        wait_gone(1, NA // 2, NA)

    scale(1, 1 - r, 1)
    span(tile, "c1a", 2, 4)

    @pl.when(r == 1)
    def _():
        wait_gone(1, NA // 2, NA)

    scale(1, 2, 1)
    span(tile, "c0a", 1, 4)
    span(z2, "c1a", 2, 4)

    @pl.when(jnp.logical_not(jnp.logical_and(r == 1, c == 1)))
    def _():
        wait_mate(1, NA // 2, NA)
        scale(1, 3, 1)

    @pl.when(c == 0)
    def _():
        span(tile, "c2a", 1, 2)

    span(tile, "c2a", 2, 4)
    span(z2, "c0a", 1, 4)
    span(z3, "c1a", 2, 4)

    @pl.when(c == 0)
    def _():
        span(z2, "c2a", 1, 2)

    span(z2, "c2a", 2, 4)

    def collect(kind, slot, stored):
        @pl.when(jnp.logical_not(stored))
        def _():
            for n in range(2):
                arrived(yr.at[kind, slot, n], y_recv.at[kind, slot, n])

    def gram_sum(kind, slots, n, rows):
        gram = decode(yr[kind, slots[0], n, rows])
        for slot in slots[1:]:
            gram += decode(yr[kind, slot, n, rows])
        return gram

    def fill(index, slots, kinds_in):
        @pl.loop(0, 3)
        def _(k):
            rows = pl.ds(pl.multiple_of(k * 32, 32), 32)
            for n in range(2):
                cols = slice(WIDE * n, WIDE * n + WIDE)
                value = gram_sum(kinds_in[0], slots, n, rows)
                if len(kinds_in) > 1:
                    value *= gram_sum(kinds_in[1], slots, n, rows)
                elif kinds_in[0] == 1:
                    value *= out[index, rows, cols]
                out[index, rows, cols] = value

    for kind in range(2):
        for h in range(2):
            collect(kind, 8 + h, h == yh)
    fill(0, (8, 9), (0, 1))
    for slot in range(4):
        collect(0, slot, jnp.logical_and(r == 1, slot == 2 + yh))
    fill(2, (0, 1, 2, 3), (0,))

    @pl.when(c == 0)
    def _():
        for slot in range(4, 8):
            collect(0, slot, yh != yh)
        fill(1, (4, 5, 6, 7), (0,))

    @pl.when(c == 1)
    def _():
        for kind in range(2):
            for h in range(2):
                collect(kind, 4 + h, h == yh)
        fill(1, (4, 5), (0, 1))

    span(z3, "c0a", 1, 4)

    @pl.when(c == 0)
    def _():
        span(z3, "c2a", 1, 2)

    span(z3, "c2a", 2, 4)

    for slot in range(4):
        collect(1, slot, jnp.logical_and(r == 1, slot == 2 + yh))
    fill(2, (0, 1, 2, 3), (1,))

    @pl.when(c == 0)
    def _():
        for slot in range(4, 8):
            collect(1, slot, yh != yh)
        fill(1, (4, 5, 6, 7), (1,))

    for kind in (0, 1):
        @pl.loop(0, kinds[kind][5])
        def _(k):
            x_copy(kind, k).wait_send()

    for k in range(1, NA):
        pair_copy(1, k).wait_send()

    @pl.when(c == 0)
    def _():
        for copy in w_copies():
            copy.wait_send()

    for step_ in range(1, 8):
        sum_copy(step_).wait_send()
    for copy in near + inv_far():
        copy.wait_send()

    on_core(1, gone, "wa", "wg")
    every(gone, "c0g", "c1g", "c2g", "c0a", "c1a", "c2a")


def on_device(acts, grads):
    dma = pltpu.SemaphoreType.DMA
    n = len(UNITS)
    slots = 8
    any_space = pl.BlockSpec(memory_space=pl.ANY)
    result = pl.pallas_call(
        kernel,
        out_shape=(
            jax.ShapeDtypeStruct((3, SEG, ROWS), F32),
            jax.ShapeDtypeStruct((ROWS, KA), BF16),
            jax.ShapeDtypeStruct((ROWS, KG), BF16),
        ),
        in_specs=[any_space, any_space],
        out_specs=(pl.BlockSpec(memory_space=pltpu.VMEM), any_space, any_space),
        scratch_shapes=[
            pltpu.VMEM((ROWS, KA), BF16),
            pltpu.VMEM((ROWS, KG), BF16),
            pltpu.VMEM((4, ROWS, HA), BF16),
            pltpu.VMEM((4, ROWS, HG), BF16),
            pltpu.VMEM((WIDE, KA), BF16),
            pltpu.VMEM((slots, 8, SEG, ROWS), F32),
            pltpu.VMEM((slots, 4, SEG, WIDE), BF16),
            pltpu.VMEM((slots, 4, 2, SEG, WIDE), BF16),
            pltpu.VMEM((slots, 4, SEG, WIDE), BF16),
            pltpu.VMEM((n, 4, SEG, WIDE), BF16),
            pltpu.VMEM((n, 4, 2, SEG, WIDE), BF16),
            pltpu.VMEM((2, 10, 2, SEG, WIDE), BF16),
            pltpu.VMEM((8, 8, ROWS), F32),
            pltpu.VMEM((6, 8, ROWS), F32),
            dma((2,)), dma((2,)), dma((NA,)), dma((NG,)), dma((NA,)), dma((NG,)),
            dma((NA,)), dma((NG,)), dma((NA,)), dma((NG,)),
            dma((NA,)), dma((NG,)), dma((NA,)), dma((NG,)),
            dma((2,)), dma((2,)), dma,
            dma((8,)), dma((8,)), dma((5,)), dma((6,)),
            dma((n, 4, 2)), dma((n, 4, 2)), dma((n, 4, 2)), dma((n, 4, 2)), dma((n, 4)), dma((2, 10, 2)),
        ],
        compiler_params=pltpu.CompilerParams(
            collective_id=0, has_side_effects=True, vmem_limit_bytes=64 * 1024 * 1024 - 65536
        ),
        cost_estimate=pl.CostEstimate(
            flops=2 * 3 * ROWS * ROWS * (KA + KG), bytes_accessed=4 * ROWS * (KA + KG), transcendentals=0
        ),
    )(acts, grads)
    return jnp.transpose(result[0], (1, 0, 2))


def solution(mesh):
    placed = (P("ex", "tp"), P("ex", "tp"))
    return jax.shard_map(
        on_device,
        mesh=mesh,
        in_specs=placed,
        out_specs=P(("ex", "tp"), None, None),
        check_vma=False,
    )
```
